32 devices in a mesh: dp: 2 (over core), expert: 16 (over z, y, x).
Axes of the slice: x: 2, y: 2, z: 4, core: 2. Of those that a mesh axis runs over, the one named last changes fastest.
Arguments:
- tokens_in: bfloat16 [4096, 2048], P(('dp', 'expert')), may hold values from -6 to 6
- grad_out: bfloat16 [4096, 2048], P(('dp', 'expert')), may hold values from -6 to 6
- routes: int32 [4096, 8], P(('dp', 'expert')), may hold values from 0 to 15, all different within a row; in each aligned block of 128 rows (0 to 127, 128 to 255, ...) at most 66 rows name the same one
- router_weight: bfloat16 [2048, 16], replicated, may hold values from -0.125 to 0.125
- w_gate: bfloat16 [16, 768, 2048], P('expert'), may hold values from -0.125 to 0.125
- w_up: bfloat16 [16, 768, 2048], P('expert'), may hold values from -0.125 to 0.125
- w_down: bfloat16 [16, 768, 2048], P('expert'), may hold values from -0.21875 to 0.21875
Outputs:
- grad_x: bfloat16 [4096, 2048], P(('dp', 'expert'))
- grad_gate: bfloat16 [16, 768, 2048], P('expert', 'dp')
- grad_up: bfloat16 [16, 768, 2048], P('expert', 'dp')
- grad_down: bfloat16 [16, 768, 2048], P('expert', 'dp')
- grad_router: float32 [2048, 16], replicated
The draws below stay inside these ranges and needn't reach their ends.
Inputs may be any that keep to these rules, and one draw needn't show every extreme that they name: `routes`: each row names 8 different experts. Among the 128 rows of one device no expert is named more than 66 times, and in every draw some expert is named exactly 66 times by the rows of some device.
All inputs are finite; a program needn't handle non-finite values.
Results may differ from the reference program's by a relative error of at most 0.009.
Values may be sent and summed in bfloat16 or wider, within the bound.
No kernel may reach another device: no remote copies, remote signals or barrier semaphores. Data moves between devices by JAX's collectives and lax.ppermute only.
A program may use at most 192 MiB of HBM per device.

```python
import math
import jax
import jax.numpy as jnp
import numpy as np
from jax import lax

D = 2048
FF = 768
TOP = 8
TOK_DEV = 128
EXPERTS = 16
CAP = 66
TOKENS = 4096
N_DP = 2
N_EXPERT = 16


def level_of(stream_key, dims, split, least, top_value):
    def one(axis_at, blocks):
        draws = jax.random.uniform(jax.random.fold_in(jax.random.fold_in(stream_key, 6), axis_at), (blocks,), jnp.float32, least / len(split), top_value / len(split))
        return jnp.repeat(jnp.exp(draws), dims[axis_at] // blocks).reshape((-1,) + (1,) * (len(dims) - axis_at - 1))

    loudness = one(*split[0])
    for cut in split[1:]:
        loudness = loudness * one(*cut)
    return loudness


def routed_block(rng, own, number, rows, number_of, top, reach, skew):
    order = jax.random.permutation(rng, number_of)
    packed, usual = load_shares(number_of, rows * top, reach, skew, True), load_shares(number_of, rows * top, reach, skew, False)
    places = jnp.arange(number_of)

    def named(lengths, offset_by):
        used = int((lengths > 0).sum())
        fixed = max(1, used // 4)
        moved = fixed + (places - fixed + offset_by * (used - fixed)) % max(1, number_of - fixed)
        return jnp.zeros((number_of,), jnp.int32).at[order[jnp.where(places < fixed, places, moved)]].set(jnp.asarray(lengths, jnp.int32))

    lengths = jnp.where(number % 4 == 0, named(packed, number // 4), named(usual, number - number // 4 - 1))
    mixed = jax.random.permutation(jax.random.fold_in(own, 3), number_of)
    giver, taker = mixed[0:number_of // 2 * 2:2], mixed[1:number_of // 2 * 2:2]
    room = jnp.minimum(lengths[giver] - 1, reach - lengths[taker]) // 2
    room = jnp.where((giver == order[0]) | (taker == order[0]) | (lengths[taker] == 0), 0, jnp.maximum(room, 0))
    moved = jax.random.randint(jax.random.fold_in(own, 4), (number_of // 2,), 0, 1 << 20) % (room + 1)
    lengths = lengths.at[giver].add(-moved).at[taker].add(moved)
    labels = jnp.searchsorted(jnp.cumsum(lengths), jnp.arange(rows * top), side="right").astype(jnp.int32)
    table = labels.reshape(top, rows).T
    table = table[jax.random.permutation(jax.random.fold_in(own, 1), rows)]
    offset_by = jax.random.randint(jax.random.fold_in(own, 2), (rows, 1), 0, top)
    return jnp.take_along_axis(table, (jnp.arange(top)[None, :] + offset_by) % top, axis=1)


def load_shares(number_of, total, most, skew, full):
    portions = [(1 << 20) // math.isqrt(standing ** skew) + 1 for standing in range(1, number_of + 1)]
    largest = most if full else min(most, max(-(-total // number_of), total * portions[0] // sum(portions)))
    least = 1 if total - largest >= number_of - 1 else 0
    counts, surplus = [largest] + [least] * (number_of - 1), total - largest - least * (number_of - 1)
    while surplus > 0:
        free = [i for i in range(1, number_of) if counts[i] < largest] or [i for i in range(1, number_of) if counts[i] < most]
        mass, remaining = sum([portions[i] for i in free]), surplus
        for i in free:
            extra = min(most - counts[i], max(1, remaining * portions[i] // mass), surplus)
            counts[i] = counts[i] + extra
            surplus = surplus - extra
    return np.array(counts)


def bell_draw(key, extent, deviation, most, split=(), kind=jnp.bfloat16):
    result = jax.random.normal(key, extent, jnp.float32) * deviation
    if len(split) > 0:
        result = level_of(key, extent, split, -0.22, 0.18) * result
    return jnp.clip(result, min=-most, max=most).astype(kind)


def setup_inputs(seed: int = 0) -> dict:
    seeds = jax.random.split(jax.random.key(seed), 8)
    tokens_in = bell_draw(seeds[0], (TOKENS, D), 1.0, 6.0, ((0, 32),))
    grad_out = bell_draw(seeds[1], (TOKENS, D), 1.0, 6.0, ((0, 32),))
    routes_keys = jax.random.split(jax.random.fold_in(seeds[2], 1), TOKENS // TOK_DEV)
    routes_turns = jax.random.permutation(jax.random.fold_in(seeds[2], 3), TOKENS // TOK_DEV)
    routes = jax.vmap(lambda own, number: routed_block(jax.random.fold_in(seeds[2], 2), own, number, TOK_DEV, EXPERTS, TOP, CAP, 2))(routes_keys, routes_turns).reshape((TOKENS, TOP))
    router_weight = bell_draw(seeds[3], (D, EXPERTS), D ** -0.5, 0.125)
    w_gate = bell_draw(seeds[4], (EXPERTS, FF, D), D ** -0.5, 0.125, ((0, 16),))
    w_up = bell_draw(seeds[5], (EXPERTS, FF, D), D ** -0.5, 0.125, ((0, 16),))
    w_down = bell_draw(seeds[6], (EXPERTS, FF, D), FF ** -0.5, 0.21875, ((0, 16),))
    return dict(tokens_in=tokens_in, grad_out=grad_out, routes=routes, router_weight=router_weight, w_gate=w_gate, w_up=w_up, w_down=w_down)


def reference(tokens_in, grad_out, routes, router_weight, w_gate, w_up, w_down):
    logits = jnp.dot(tokens_in, router_weight, preferred_element_type=jnp.float32)
    chosen = jnp.take_along_axis(logits, routes, axis=1)
    probs = jax.nn.softmax(chosen, axis=1)
    pair_count = TOKENS * TOP
    limit = N_DP * N_EXPERT * CAP
    flat_routes = routes.reshape(-1)
    flat_probs = probs.reshape(-1)
    pair_index = jnp.arange(pair_count, dtype=jnp.int32)

    def per_expert(carry, expert_id):
        part_sum, weighted_flat = carry
        member = flat_routes == expert_id
        position = jnp.cumsum(member.astype(jnp.int32)) - 1
        target = jnp.where(member, position, limit).astype(jnp.int32)
        index = jnp.zeros((limit,), jnp.int32).at[target].set(pair_index, mode="drop")
        valid = jnp.arange(limit, dtype=jnp.int32) < jnp.sum(member.astype(jnp.int32))
        token_of = index // TOP
        rows_x = jnp.where(valid[:, None], tokens_in[token_of], jnp.zeros((), jnp.bfloat16))
        gate_prob = jnp.where(valid, flat_probs[index], jnp.float32(0.0))
        rows_s = (gate_prob[:, None] * grad_out[token_of].astype(jnp.float32)).astype(jnp.bfloat16)
        gate_w = w_gate[expert_id]
        up_w = w_up[expert_id]
        down_w = w_down[expert_id]
        pre_gate = jnp.dot(rows_x, gate_w.T, preferred_element_type=jnp.float32)
        pre_up = jnp.dot(rows_x, up_w.T, preferred_element_type=jnp.float32)
        sig = jax.nn.sigmoid(pre_gate)
        act = pre_gate * sig
        hidden = (act * pre_up).astype(jnp.bfloat16)
        grad_hidden = jnp.dot(rows_s, down_w.T, preferred_element_type=jnp.float32)
        weighted = jnp.sum(hidden.astype(jnp.float32) * grad_hidden, axis=1)
        grad_pg = (grad_hidden * pre_up * sig * (1.0 + pre_gate * (1.0 - sig))).astype(jnp.bfloat16)
        grad_pu = (grad_hidden * act).astype(jnp.bfloat16)
        part = (jnp.dot(grad_pg, gate_w, preferred_element_type=jnp.float32)
                + jnp.dot(grad_pu, up_w, preferred_element_type=jnp.float32)).astype(jnp.bfloat16)
        drop_index = jnp.where(valid, index, pair_count).astype(jnp.int32)
        drop_token = jnp.where(valid, token_of, TOKENS).astype(jnp.int32)
        part_sum = part_sum.at[drop_token].add(part.astype(jnp.float32), mode="drop")
        weighted_flat = weighted_flat.at[drop_index].set(weighted, mode="drop")
        g_gate = jnp.dot(grad_pg.T, rows_x, preferred_element_type=jnp.float32).astype(jnp.bfloat16)
        g_up = jnp.dot(grad_pu.T, rows_x, preferred_element_type=jnp.float32).astype(jnp.bfloat16)
        g_down = jnp.dot(hidden.T, rows_s, preferred_element_type=jnp.float32).astype(jnp.bfloat16)
        return (part_sum, weighted_flat), (g_gate, g_up, g_down)

    start = (jnp.zeros((TOKENS, D), jnp.float32), jnp.zeros((pair_count,), jnp.float32))
    (part_sum, weighted_flat), (grad_gate, grad_up, grad_down) = lax.scan(
        per_expert, start, jnp.arange(EXPERTS, dtype=jnp.int32))
    weighted = weighted_flat.reshape(TOKENS, TOP)
    dchosen = weighted - probs * jnp.sum(weighted, axis=1, keepdims=True)
    columns = jnp.arange(EXPERTS, dtype=jnp.int32)
    dlogits = jnp.sum(dchosen[:, :, None] * (routes[:, :, None] == columns[None, None, :]).astype(jnp.float32), axis=1).astype(jnp.bfloat16)
    grad_x = (part_sum + jnp.dot(dlogits, router_weight.T, preferred_element_type=jnp.float32)).astype(jnp.bfloat16)
    grad_router = jnp.dot(tokens_in.T, dlogits, preferred_element_type=jnp.float32) / TOK_DEV
    return grad_x, grad_gate, grad_up, grad_down, grad_router
```

```python
import functools

import jax
import jax.numpy as jnp
from jax import lax
from jax.experimental import pallas as pl
from jax.experimental.pallas import tpu as pltpu
from jax.sharding import PartitionSpec as P

LINE = 4
EXTRA = 16
MIB = 1 << 20
F32 = jnp.float32
BF16 = jnp.bfloat16


def dot(a, b, contract):
    return lax.dot_general(a, b, (contract, ((), ())), preferred_element_type=F32)


def params(limit=48):
    return pltpu.CompilerParams(vmem_limit_bytes=limit * MIB)


def cost(flops, size):
    return pl.CostEstimate(flops=int(flops), bytes_accessed=int(size), transcendentals=0)


def whole():
    return pl.BlockSpec(memory_space=pltpu.VMEM)


def smem():
    return pl.BlockSpec(memory_space=pltpu.SMEM)


def gate_kernel(routes_ref, x_ref, router_ref, out_ref):
    logits = dot(router_ref[...], x_ref[...], ((1,), (1,)))
    row = lax.broadcasted_iota(jnp.int32, logits.shape, 0)
    member = row == routes_ref[0:1, :]
    for k in range(1, routes_ref.shape[0]):
        member = member | (row == routes_ref[k : k + 1, :])
    top = jnp.max(jnp.where(member, logits, -jnp.inf), axis=0, keepdims=True)
    weight = jnp.where(member, jnp.exp(logits - top), 0.0)
    out_ref[...] = jnp.where(member, weight / jnp.sum(weight, axis=0, keepdims=True), -1.0)


def rank_of(prob):
    count = prob.shape[1]
    earlier = lax.broadcasted_iota(jnp.int32, (count, count), 0) < lax.broadcasted_iota(
        jnp.int32, (count, count), 1
    )
    member = prob >= 0.0
    rank = dot(member.astype(F32).astype(BF16), earlier.astype(F32).astype(BF16), ((1,), (0,)))
    return jnp.where(member, rank, -1.0)


def slots(rank_row, count, first):
    row = lax.broadcasted_iota(jnp.int32, (count, rank_row.shape[1]), 0).astype(F32)
    return (row + first == rank_row).astype(F32)


def extra_slots(rank_row, main, r):
    row = lax.broadcasted_iota(jnp.int32, (EXTRA, rank_row.shape[1]), 0).astype(F32) - 2.0 * r
    return ((row >= 0.0) & (row < 2.0) & (row + main == rank_row)).astype(F32)


def compact_kernel(plane, main, scaled, extra, place_ref, *refs):
    blocks = LINE if extra else 1
    z, q, end = place_ref[0], place_ref[1], place_ref[2]
    refs = list(refs)
    prob_refs = [refs.pop(0) for _ in range(blocks)]
    outs = refs[-1 - plane : -1]
    rank_ref = refs[-1]
    cands = refs[: -1 - plane]
    if extra:
        groups = [cands[0:1], cands[1:2], cands[2:4], cands[4:6]]
    else:
        groups = [cands]
    rows = []
    for group in groups:
        block = group[0][...]
        if len(group) == 2:
            block = jnp.where(end > 0, block, group[1][...])
        rows.append(block)

    def gathered(picks, probs, block):
        value = dot(jnp.concatenate(picks, axis=0).astype(BF16), block, ((1,), (0,)))
        if scaled:
            factor = [jnp.sum(a * b, axis=1, keepdims=True) for a, b in zip(picks, probs)]
            value = value * jnp.concatenate(factor, axis=0)
        return value

    tail = None
    for r in range(blocks):
        rank_ref[...] = rank_of(prob_refs[r][...])
        picks, probs, more = [], [], []
        for s in range(plane):
            expert = z * plane + (q ^ s)
            rank_row = rank_ref[pl.ds(expert, 1), :]
            probs.append(prob_refs[r][pl.ds(expert, 1), :])
            picks.append(slots(rank_row, main, 0.0))
            if extra:
                more.append(extra_slots(rank_row, float(main), r))
        if r == blocks - 1:
            value = gathered(picks, probs, rows[r])
            for s in range(plane):
                outs[s][0:main, :] = value[s * main : (s + 1) * main].astype(BF16)
        if extra:
            value = gathered(more, probs, rows[r])
            tail = value if tail is None else tail + value
    if extra:
        for s in range(plane):
            outs[s][main : main + EXTRA, :] = tail[s * EXTRA : (s + 1) * EXTRA].astype(BF16)


def compact(place, probs, cands, plane, main, scaled, extra):
    experts, count = probs[0].shape
    width = cands[0].shape[1]
    height = main + (EXTRA if extra else 0)
    return pl.pallas_call(
        functools.partial(compact_kernel, plane, main, scaled, extra),
        out_shape=[jax.ShapeDtypeStruct((height, width), BF16)] * plane,
        in_specs=[smem()] + [whole()] * (len(probs) + len(cands)),
        out_specs=[whole()] * plane,
        scratch_shapes=[pltpu.VMEM((experts, count), F32)],
        compiler_params=params(),
        cost_estimate=cost(
            2 * plane * height * count * width, 2 * width * (len(cands) * count + plane * height)
        ),
    )(place, *probs, *cands)


def expert_kernel(plane, *refs):
    xs, ss = refs[:plane], refs[plane : 2 * plane]
    gate_ref, up_ref, down_ref = refs[2 * plane : 2 * plane + 3]
    parts = refs[2 * plane + 3 : 3 * plane + 3]
    hidden_ref, gg_ref, gu_ref, rows_x, rows_s, score_ref, total, score = refs[3 * plane + 3 :]
    height = xs[0].shape[0]
    step, last = pl.program_id(0), pl.num_programs(0) - 1

    @pl.when(step == 0)
    def _():
        for s in range(plane):
            rows_x[s * height : (s + 1) * height, :] = xs[s][...]
            rows_s[s * height : (s + 1) * height, :] = ss[s][...]
        total[...] = jnp.zeros_like(total)
        score[...] = jnp.zeros_like(score)

    gate_w, up_w, down_w = gate_ref[0], up_ref[0], down_ref[0]
    pre_gate = dot(rows_x[...], gate_w, ((1,), (1,)))
    pre_up = dot(rows_x[...], up_w, ((1,), (1,)))
    grad_hidden = dot(rows_s[...], down_w, ((1,), (1,)))
    sig = jax.nn.sigmoid(pre_gate)
    act = pre_gate * sig
    hidden = (act * pre_up).astype(BF16)
    grad_pg = (grad_hidden * pre_up * sig * (1.0 + pre_gate * (1.0 - sig))).astype(BF16)
    grad_pu = (grad_hidden * act).astype(BF16)
    hidden_ref[...] = hidden
    gg_ref[...] = grad_pg
    gu_ref[...] = grad_pu
    score[...] += jnp.sum(hidden.astype(F32) * grad_hidden, axis=1, keepdims=True)
    total[...] += dot(grad_pg, gate_w, ((1,), (0,))) + dot(grad_pu, up_w, ((1,), (0,)))

    @pl.when(step == last)
    def _():
        for s in range(plane):
            parts[s][...] = total[s * height : (s + 1) * height, :].astype(BF16)
        spread = jnp.broadcast_to(score[...], (score.shape[0], 128))
        score_ref[...] = spread.T[0:8, :]


def expert(xs, ss, gate_w, up_w, down_w):
    plane = len(xs)
    height, width = xs[0].shape
    rows = plane * height
    hid = gate_w.shape[1]
    tile = 256 if hid % 256 == 0 else hid
    wspec = pl.BlockSpec((1, tile, width), lambda i: (0, i, 0))
    part = pl.BlockSpec((height, width), lambda i: (0, 0))
    narrow = pl.BlockSpec((rows, tile), lambda i: (0, i))
    full = pl.BlockSpec((rows, width), lambda i: (0, 0))
    out = pl.pallas_call(
        functools.partial(expert_kernel, plane),
        grid=(hid // tile,),
        out_shape=[jax.ShapeDtypeStruct((height, width), BF16)] * plane
        + [jax.ShapeDtypeStruct((rows, hid), BF16)] * 3
        + [jax.ShapeDtypeStruct((rows, width), BF16)] * 2
        + [jax.ShapeDtypeStruct((8, rows), F32)],
        in_specs=[part] * (2 * plane) + [wspec] * 3,
        out_specs=[part] * plane
        + [narrow] * 3
        + [full] * 2
        + [pl.BlockSpec((8, rows), lambda i: (0, 0))],
        scratch_shapes=[pltpu.VMEM((rows, width), F32), pltpu.VMEM((rows, 1), F32)],
        compiler_params=params(),
        cost_estimate=cost(10 * rows * width * hid, 6 * hid * width + 10 * rows * width),
    )(*xs, *ss, gate_w, up_w, down_w)
    return out[:plane], out[plane : plane + 3], out[plane + 3 : plane + 5], out[plane + 5]


def weight_kernel(chunks, added, half_ref, *refs):
    xs, ss = refs[:chunks], refs[chunks : 2 * chunks]
    hs, ggs, gus = (refs[(2 + i) * chunks : (3 + i) * chunks] for i in range(3))
    refs = refs[5 * chunks :]
    for i, (left, right) in enumerate(((ggs, xs), (gus, xs), (hs, ss))):
        total = dot(left[0][...], right[0][...], ((0,), (0,)))
        for r in range(1, chunks):
            total = total + dot(left[r][...], right[r][...], ((0,), (0,)))
        if added:
            refs[3 + i][0] = (total + refs[i][...].astype(F32)).astype(BF16)
        else:
            refs[i][...] = total.astype(BF16)


def weight_grads(half, xs, ss, hs, ggs, gus, parts, other):
    chunks = len(xs)
    width = xs[0].shape[1]
    rows = hs[0].shape[1] // parts
    fixed = [pl.BlockSpec(a.shape, lambda i, ref: (0, 0)) for a in (*xs, *ss)]
    cut = [pl.BlockSpec((a.shape[0], rows), lambda i, ref: (0, ref[0])) for a in (*hs, *ggs, *gus)]
    flat = pl.BlockSpec((rows, width), lambda i, ref: (0, 0))
    if other is None:
        out_spec, shape, given = flat, (rows, width), ()
    else:
        out_spec, shape, given = (
            pl.BlockSpec((1, rows, width), lambda i, ref: (0, 0, 0)),
            (1, rows, width),
            tuple(other),
        )
    count = sum(a.shape[0] for a in xs)
    return pl.pallas_call(
        functools.partial(weight_kernel, chunks, other is not None),
        grid_spec=pltpu.PrefetchScalarGridSpec(
            num_scalar_prefetch=1,
            grid=(1,),
            in_specs=fixed + cut + [flat] * len(given),
            out_specs=[out_spec] * 3,
        ),
        out_shape=[jax.ShapeDtypeStruct(shape, BF16)] * 3,
        compiler_params=params(60),
        cost_estimate=cost(6 * count * rows * width, 4 * count * width + 6 * rows * width),
    )(half, *xs, *ss, *hs, *ggs, *gus, *given)


def scatter_kernel(plane, main, r, added, last, place_ref, prob_ref, *refs):
    refs = list(refs)
    rows_ref, more_ref, rank_ref = refs[-3:]
    out_ref = refs[-4]
    backs, refs = refs[:plane], refs[plane:-4]
    tails, refs = refs[:plane], refs[plane:]
    z, q = place_ref[0], place_ref[1]
    rank_ref[...] = rank_of(prob_ref[...])
    picks, more = [], []
    for s in range(plane):
        rank_row = rank_ref[pl.ds(z * plane + (q ^ s), 1), :]
        picks.append(slots(rank_row, main, 0.0))
        more.append(extra_slots(rank_row, float(main), r))
        rows_ref[s * main : (s + 1) * main, :] = backs[s][...]
        more_ref[s * EXTRA : (s + 1) * EXTRA, :] = tails[s][...]
    total = dot(jnp.concatenate(picks, axis=0).astype(BF16), rows_ref[...], ((0,), (0,)))
    total = total + dot(jnp.concatenate(more, axis=0).astype(BF16), more_ref[...], ((0,), (0,)))
    for i in range(added):
        total = total + refs[i][...].astype(F32)
    if last:
        total = total + dot(refs[added][...], refs[added + 1][...], ((0,), (0,)))
    out_ref[...] = total.astype(BF16)


def scatter(place, prob, backs, tails, main, r, added, router=()):
    plane = len(backs)
    width = backs[0].shape[1]
    experts, count = prob.shape
    head = pl.BlockSpec((main, width), lambda i: (0, 0))
    tail = pl.BlockSpec((EXTRA, width), lambda i: (main // EXTRA, 0))
    dense = pl.BlockSpec((count, width), lambda i: (0, 0))
    fixed = lambda a: pl.BlockSpec(a.shape, lambda i: (0, 0))
    return pl.pallas_call(
        functools.partial(scatter_kernel, plane, main, r, len(added), len(router) > 0),
        grid=(1,),
        out_shape=jax.ShapeDtypeStruct((count, width), BF16),
        in_specs=[smem(), fixed(prob)]
        + [head] * plane
        + [tail] * plane
        + [dense] * len(added)
        + [fixed(a) for a in router],
        out_specs=dense,
        scratch_shapes=[
            pltpu.VMEM((plane * main, width), BF16),
            pltpu.VMEM((plane * EXTRA, width), BF16),
            pltpu.VMEM((experts, count), F32),
        ],
        compiler_params=params(),
        cost_estimate=cost(2 * plane * (main + EXTRA) * count * width, 6 * plane * main * width),
    )(place, prob, *backs, *tails, *added, *router)


def router_kernel(prob_ref, score_ref, x_ref, dlogits_ref, term_ref, dense_ref):
    prob = prob_ref[...]
    rank = rank_of(prob)
    member = prob >= 0.0
    score = score_ref[...]
    high = score.astype(BF16)
    rest = score - high.astype(F32)
    mid = rest.astype(BF16)
    low = (rest - mid.astype(F32)).astype(BF16)
    for e in range(prob.shape[0]):
        pick = slots(rank[e : e + 1, :], score.shape[1], 0.0).astype(BF16)
        value = dot(high[e : e + 1, :], pick, ((1,), (0,)))
        value = value + dot(mid[e : e + 1, :], pick, ((1,), (0,)))
        dense_ref[e : e + 1, :] = value + dot(low[e : e + 1, :], pick, ((1,), (0,)))
    weighted = dense_ref[...]
    both = weighted - prob * jnp.sum(weighted, axis=0, keepdims=True)
    dlogits = jnp.where(member, both, 0.0).astype(BF16)
    dlogits_ref[...] = dlogits
    term_ref[...] = dot(dlogits, x_ref[...], ((1,), (0,)))


def router_grads(prob, score, x):
    experts, count = prob.shape
    width = x.shape[1]
    return pl.pallas_call(
        router_kernel,
        out_shape=[
            jax.ShapeDtypeStruct((experts, count), BF16),
            jax.ShapeDtypeStruct((experts, width), F32),
        ],
        in_specs=[whole()] * 3,
        out_specs=[whole()] * 2,
        scratch_shapes=[pltpu.VMEM((experts, count), F32)],
        compiler_params=params(),
        cost_estimate=cost(2 * experts * count * (width + 3 * count), 2 * count * width),
    )(prob, score, x)


def local(tokens_in, grad_out, routes, router_weight, w_gate, w_up, w_down):
    tok_count, width = tokens_in.shape
    top_count = routes.shape[1]
    experts = router_weight.shape[1]
    main = tok_count * top_count // experts
    cap = main + 2
    plane = experts // LINE
    me = lax.axis_index("expert")
    core = lax.axis_index("dp")
    z, q = me // plane, me % plane
    end = ((z == 0) | (z == LINE - 1)).astype(jnp.int32)
    place = jnp.stack([z, q, end]).astype(jnp.int32)
    router_t = router_weight.T

    def line(pairs):
        return [(a * plane + i, b * plane + i) for a, b in pairs for i in range(plane)]

    pair_swap = line([(0, 1), (1, 0), (2, 3), (3, 2)])
    mid_swap = line([(1, 2), (2, 1)])
    outward = line([(1, 0), (2, 3)])
    inward = line([(0, 1), (3, 2)])
    send = lambda a, perm: lax.ppermute(a, "expert", perm)
    across = lambda a, bit: send(a, [(i, i ^ bit) for i in range(experts)])

    prob = pl.pallas_call(
        gate_kernel,
        out_shape=jax.ShapeDtypeStruct((experts, tok_count), F32),
        in_specs=[whole()] * 3,
        out_specs=whole(),
        compiler_params=params(),
        cost_estimate=cost(2 * experts * tok_count * width, 2 * tok_count * width),
    )(routes.T, tokens_in, router_t)
    probs = [prob] + [across(prob, r * plane) for r in range(1, LINE)]

    def along(a):
        near, mid = send(a, pair_swap), send(a, mid_swap)
        near2, mid2 = send(mid, outward), send(near, mid_swap)
        far = send(mid2, outward)
        return [(a,), (near,), (near2, mid2), (far, mid)]

    cand_x, cand_g = along(tokens_in), along(grad_out)

    def spread(cands, r, scaled):
        extra = r == LINE - 1
        if extra:
            given = [c for group in cands for c in group]
            rows = compact(place, probs, given, plane, main, scaled, True)
        else:
            rows = compact(place, probs[r : r + 1], cands[r], plane, main, scaled, False)
        return [rows[0]] + [across(rows[s], s) for s in range(1, plane)]

    parts, narrow, rows, scores = {}, {}, {}, {}
    for r in (0, 1, 3, 2):
        x_rows, s_rows = spread(cand_x, r, False), spread(cand_g, r, True)
        parts[r], narrow[r], rows[r], scores[r] = expert(x_rows, s_rows, w_gate, w_up, w_down)

    heads = [scores[r][0].reshape(plane, -1) for r in range(LINE)]
    tails = heads[-1][:, main : main + 2 * LINE].reshape(plane, LINE, 2).transpose(1, 0, 2)
    heads = jnp.stack([h[:, :main] for h in heads])
    packed = jnp.concatenate([heads, tails], axis=2).reshape(experts, cap)
    packed = jnp.pad(packed, ((0, 0), (0, tok_count - cap)))
    packed = packed[jnp.arange(experts) ^ me]
    score = lax.all_to_all(packed, "expert", split_axis=0, concat_axis=0, tiled=True)
    dlogits, term = router_grads(prob, score, tokens_in)
    for bit in range(experts.bit_length() - 1):
        term = term + across(term, 1 << bit)
    term = term + lax.ppermute(term, "dp", [(0, 1), (1, 0)])
    grad_router = term.T / tok_count

    back = {}
    for r in (3, 2, 1, 0):
        back[r] = [parts[r][0]] + [across(parts[r][s], s) for s in range(1, plane)]
    extra = back[LINE - 1]
    join = lambda r, added, router=(): scatter(
        place, probs[r], back[r], extra, main, r, added, router
    )
    far = join(3, [])
    sum2 = join(2, [send(far, inward)])
    far = (far.astype(F32) + send(sum2, inward).astype(F32)).astype(BF16)
    sum1 = join(1, [send(sum2, mid_swap)])
    grad_x = join(0, [send(sum1, pair_swap), send(far, mid_swap)], (dlogits, router_t))

    order = range(LINE)
    given = (
        [rows[r][0] for r in order],
        [rows[r][1] for r in order],
        [narrow[r][0] for r in order],
        [narrow[r][1] for r in order],
        [narrow[r][2] for r in order],
    )
    replicas = 2
    half = core.reshape(1).astype(jnp.int32)
    gone = weight_grads(1 - half, *given, replicas, None)
    other = [lax.ppermute(a, "dp", [(0, 1), (1, 0)]) for a in gone]
    grad_gate, grad_up, grad_down = weight_grads(half, *given, replicas, other)
    return (grad_x, grad_gate, grad_up, grad_down, grad_router)


def solution(mesh):
    return jax.shard_map(
        local,
        mesh=mesh,
        in_specs=(
            P(("dp", "expert"), None),
            P(("dp", "expert"), None),
            P(("dp", "expert"), None),
            P(),
            P("expert", None, None),
            P("expert", None, None),
            P("expert", None, None),
        ),
        out_specs=(
            P(("dp", "expert"), None),
            P("expert", "dp", None),
            P("expert", "dp", None),
            P("expert", "dp", None),
            P(),
        ),
        check_vma=False,
    )
```

```python
import functools

import jax
import jax.numpy as jnp
from jax import lax
from jax.experimental import pallas as pl
from jax.experimental.pallas import tpu as pltpu
from jax.sharding import PartitionSpec as P

LINE = 4
OVER = 2
EXTRA = 16
MIB = 1 << 20
SPEED = 1.1e9
F32 = jnp.float32
BF16 = jnp.bfloat16


def dot(a, b, contract):
    return lax.dot_general(a, b, (contract, ((), ())), preferred_element_type=F32)


def hbm():
    return pl.BlockSpec(memory_space=pl.ANY)


def whole():
    return pl.BlockSpec(memory_space=pltpu.VMEM)


def smem():
    return pl.BlockSpec(memory_space=pltpu.SMEM)


def call(kernel, operands, in_specs, out_shape, out_specs, after, micros, scratch=()):
    count, more = len(operands), len(after)

    def body(*refs):
        kernel(*refs[:count], *refs[count + more :])

    return pl.pallas_call(
        body,
        out_shape=out_shape,
        in_specs=list(in_specs) + [hbm()] * more,
        out_specs=out_specs,
        scratch_shapes=scratch,
        compiler_params=pltpu.CompilerParams(vmem_limit_bytes=60 * MIB),
        cost_estimate=pl.CostEstimate(
            flops=int(micros * SPEED), bytes_accessed=1024, transcendentals=0
        ),
    )(*operands, *after)


def like(shape, kind=BF16):
    return jax.ShapeDtypeStruct(shape, kind)


def group(size):
    return -(-size // 16) * 16


def gate_kernel(routes_ref, x_ref, g_ref, router_ref, prob_ref, out_ref):
    logits = dot(router_ref[...], x_ref[...], ((1,), (1,)))
    row = lax.broadcasted_iota(jnp.int32, logits.shape, 0)
    member = row == routes_ref[0:1, :]
    for k in range(1, routes_ref.shape[0]):
        member = member | (row == routes_ref[k : k + 1, :])
    top = jnp.max(jnp.where(member, logits, -jnp.inf), axis=0, keepdims=True)
    weight = jnp.where(member, jnp.exp(logits - top), 0.0)
    prob = jnp.where(member, weight / jnp.sum(weight, axis=0, keepdims=True), -1.0)
    prob_ref[...] = prob
    experts, count = prob.shape
    out_ref[0:count, :] = x_ref[...]
    out_ref[count : 2 * count, :] = g_ref[...]
    rest = prob
    for k in range(3):
        piece = rest.astype(BF16)
        rest = rest - piece.astype(F32)
        out_ref[2 * count : 2 * count + experts, k * count : (k + 1) * count] = piece
    tail = out_ref.shape[1] - 3 * count
    out_ref[2 * count : 2 * count + experts, 3 * count :] = jnp.zeros((experts, tail), BF16)


def rank_of(prob):
    count = prob.shape[1]
    earlier = lax.broadcasted_iota(jnp.int32, (count, count), 0) < lax.broadcasted_iota(
        jnp.int32, (count, count), 1
    )
    member = prob >= 0.0
    rank = dot(member.astype(F32).astype(BF16), earlier.astype(F32).astype(BF16), ((1,), (0,)))
    return jnp.where(member, rank, -1.0)


def slots(rank_row, count):
    row = lax.broadcasted_iota(jnp.int32, (count, rank_row.shape[1]), 0).astype(F32)
    return (row == rank_row).astype(F32)


def extra_slots(rank_row, main, r, shift):
    row = lax.broadcasted_iota(jnp.int32, (EXTRA, rank_row.shape[1]), 0).astype(F32)
    row = row - float(shift + OVER * r)
    return ((row >= 0.0) & (row < OVER) & (row + main == rank_row)).astype(F32)


def compact_kernel(plane, main, r, cands, place_ref, *refs):
    z, q, end = place_ref[0], place_ref[1], place_ref[2]
    given, refs = refs[:cands], refs[cands:]
    if r > 0:
        tail_in, refs = refs[0], refs[1:]
    outs, refs = refs[:plane], refs[plane:]
    prob_ref, tail_ref, rank_ref = refs
    experts, count = prob_ref.shape
    block = given[0][...]
    if cands == 2:
        block = jnp.where(end > 0, block, given[1][...])
    rows_x, rows_s = block[0:count], block[count : 2 * count]
    pieces = [
        block[2 * count : 2 * count + experts, k * count : (k + 1) * count].astype(F32)
        for k in range(3)
    ]
    prob_ref[...] = (pieces[0] + pieces[1]) + pieces[2]
    rank_ref[...] = rank_of(prob_ref[...])
    picks, more_x, more_s, factor, more_factor = [], [], [], [], []
    for s in range(plane):
        expert = z * plane + (q ^ s)
        rank_row = rank_ref[pl.ds(expert, 1), :]
        prob_row = prob_ref[pl.ds(expert, 1), :]
        picks.append(slots(rank_row, main))
        more_x.append(extra_slots(rank_row, main, r, 0))
        more_s.append(extra_slots(rank_row, main, r, LINE * OVER))
        factor.append(jnp.sum(picks[-1] * prob_row, axis=1, keepdims=True))
        more_factor.append(jnp.sum(more_s[-1] * prob_row, axis=1, keepdims=True))
    pick = jnp.concatenate(picks, axis=0).astype(BF16)
    value_x = dot(pick, rows_x, ((1,), (0,)))
    value_s = dot(pick, rows_s, ((1,), (0,))) * jnp.concatenate(factor, axis=0)
    tail = dot(jnp.concatenate(more_x, axis=0).astype(BF16), rows_x, ((1,), (0,)))
    tail_s = dot(jnp.concatenate(more_s, axis=0).astype(BF16), rows_s, ((1,), (0,)))
    tail = tail + tail_s * jnp.concatenate(more_factor, axis=0)
    if r > 0:
        tail = tail + tail_in[...].astype(F32)
    tail_ref[...] = tail.astype(BF16)
    for s in range(plane):
        part = slice(s * main, (s + 1) * main)
        outs[s][0:main, :] = value_x[part].astype(BF16)
        outs[s][main : 2 * main, :] = value_s[part].astype(BF16)
        if r == LINE - 1:
            outs[s][2 * main :, :] = tail[s * EXTRA : (s + 1) * EXTRA].astype(BF16)


def compact(place, cands, tail, plane, experts, count, main, r, after):
    width = cands[0].shape[1]
    height = 2 * main + (EXTRA if r == LINE - 1 else 0)
    operands = [place, *cands] + ([] if tail is None else [tail])
    out = call(
        functools.partial(compact_kernel, plane, main, r, len(cands)),
        operands,
        [smem()] + [whole()] * (len(operands) - 1),
        [like((height, width))] * plane
        + [like((experts, count), F32), like((plane * EXTRA, width))],
        [whole()] * (plane + 2),
        after,
        3.0,
        [pltpu.VMEM((experts, count), F32)],
    )
    return out[:plane], out[plane], out[plane + 1]


def expert_kernel(plane, main, tile, last, *refs):
    ins, weights, refs = refs[:plane], refs[plane : plane + 3], refs[plane + 3 :]
    if last:
        earlier, refs = refs[: LINE - 1], refs[LINE - 1 :]
    parts, narrow, score_ref = refs[:plane], refs[plane : plane + 3], refs[plane + 3]
    refs = refs[plane + 4 :]
    if last:
        tails, refs = refs[:2], refs[2:]
        ebuf, e_sem, t_sem = refs[-3:]
    rows_x, rows_s, wbuf, nbuf, pbuf, row_sem, w_sem, n_sem, p_sem = refs[:9]
    hid, width = wbuf.shape[1:]
    tiles = hid // tile
    base = plane * main
    over = LINE * OVER

    row_copies = []
    for s in range(plane):
        own = pl.ds(s * main, main)
        for i, target in enumerate((rows_x, rows_s)):
            row_copies.append(
                pltpu.make_async_copy(
                    ins[s].at[pl.ds(i * main, main), :], target.at[own, :], row_sem.at[i, s]
                )
            )
        if last:
            row_copies.append(
                pltpu.make_async_copy(
                    ins[s].at[pl.ds(2 * main, EXTRA), :],
                    ebuf.at[pl.ds(s * EXTRA, EXTRA), :],
                    e_sem.at[s],
                )
            )
    w_copies = [
        [
            pltpu.make_async_copy(
                weights[i].at[0, pl.ds(f * tile, tile), :],
                wbuf.at[i, pl.ds(f * tile, tile), :],
                w_sem.at[i, f],
            )
            for i in range(3)
        ]
        for f in range(tiles)
    ]
    for copy in row_copies:
        copy.start()
    for part in w_copies:
        for copy in part:
            copy.start()
    for copy in row_copies:
        copy.wait()
    stores = []
    if last:
        extra = ebuf[...].astype(F32)
        first = [extra[s * EXTRA : s * EXTRA + over] for s in range(plane)]
        second = [extra[s * EXTRA + over : s * EXTRA + 2 * over] for s in range(plane)]
        rows_x[base:, :] = jnp.concatenate(first, axis=0).astype(BF16)
        rows_s[base:, :] = jnp.concatenate(second, axis=0).astype(BF16)
        for i, source in enumerate((rows_x, rows_s)):
            stores.append(
                pltpu.make_async_copy(
                    source.at[pl.ds(base, plane * over), :], tails[i], t_sem.at[i]
                )
            )
            stores[-1].start()

    score = jnp.zeros((rows_x.shape[0], 1), F32)
    for f in range(tiles):
        cut = slice(f * tile, (f + 1) * tile)
        for copy in w_copies[f]:
            copy.wait()
        pre_gate = dot(rows_x[...], wbuf[0, cut, :], ((1,), (1,)))
        pre_up = dot(rows_x[...], wbuf[1, cut, :], ((1,), (1,)))
        grad_hidden = dot(rows_s[...], wbuf[2, cut, :], ((1,), (1,)))
        sig = jax.nn.sigmoid(pre_gate)
        act = pre_gate * sig
        hidden = (act * pre_up).astype(BF16)
        nbuf[0, :, cut] = hidden
        nbuf[1, :, cut] = (grad_hidden * pre_up * sig * (1.0 + pre_gate * (1.0 - sig))).astype(BF16)
        nbuf[2, :, cut] = (grad_hidden * act).astype(BF16)
        score = score + jnp.sum(hidden.astype(F32) * grad_hidden, axis=1, keepdims=True)
    for i in range(3):
        stores.append(pltpu.make_async_copy(nbuf.at[i], narrow[i], n_sem.at[i]))
        stores[-1].start()
    step = min(width, 512)
    for n in range(0, width, step):
        cut = slice(n, n + step)
        total = dot(nbuf[1], wbuf[0, :, cut], ((1,), (0,)))
        total = total + dot(nbuf[2], wbuf[1, :, cut], ((1,), (0,)))
        pbuf[0:base, cut] = total[0:base].astype(BF16)
        if last:
            blank = jnp.zeros((EXTRA - over, step), F32)
            for s in range(plane):
                more = total[base + s * over : base + (s + 1) * over]
                more = jnp.concatenate([more, blank], axis=0).astype(BF16)
                pbuf[base + s * EXTRA : base + (s + 1) * EXTRA, cut] = more
    for s in range(plane):
        stores.append(
            pltpu.make_async_copy(
                pbuf.at[pl.ds(s * main, main), :],
                parts[s].at[pl.ds(0, main), :],
                p_sem.at[0, s],
            )
        )
        stores[-1].start()
        if last:
            stores.append(
                pltpu.make_async_copy(
                    pbuf.at[pl.ds(base + s * EXTRA, EXTRA), :],
                    parts[s].at[pl.ds(main, EXTRA), :],
                    p_sem.at[1, s],
                )
            )
            stores[-1].start()

    def lanes(column, shift, width=128):
        shape = (column.shape[0], width)
        row = lax.broadcasted_iota(jnp.int32, shape, 0) + shift
        lane = lax.broadcasted_iota(jnp.int32, shape, 1)
        return jnp.sum(jnp.where(row == lane, column, 0.0), axis=0, keepdims=True)

    own = [lanes(score[s * main : (s + 1) * main], 0) for s in range(plane)]
    if not last:
        score_ref[...] = jnp.concatenate(own, axis=0)
    else:
        lane = lax.broadcasted_iota(jnp.int32, (1, 128), 1)
        over_rows = [
            lanes(score[base + s * over : base + (s + 1) * over], main) for s in range(plane)
        ]
        for r in range(LINE):
            for s in range(plane):
                value = own[s] if r == LINE - 1 else earlier[r][s : s + 1, :]
                for j in range(OVER):
                    at = main + OVER * r + j
                    one = jnp.sum(jnp.where(lane == at, over_rows[s], 0.0), axis=1, keepdims=True)
                    value = jnp.where(lane == main + j, one, value)
                score_ref[r * plane + s : r * plane + s + 1, :] = value
    for copy in stores:
        copy.wait()


def expert(ins, weights, main, earlier, after):
    plane = len(ins)
    width = ins[0].shape[1]
    last = len(earlier) > 0
    hid = weights[0].shape[1]
    base, over = plane * main, LINE * OVER
    rows = base + (plane * over if last else 0)
    spread = base + (plane * EXTRA if last else 0)
    tile = 256 if hid % 256 == 0 else hid
    height = main + (EXTRA if last else 0)
    scratch = [
        pltpu.VMEM((rows, width), BF16),
        pltpu.VMEM((rows, width), BF16),
        pltpu.VMEM((3, hid, width), BF16),
        pltpu.VMEM((3, rows, hid), BF16),
        pltpu.VMEM((spread, width), BF16),
        pltpu.SemaphoreType.DMA((2, plane)),
        pltpu.SemaphoreType.DMA((3, hid // tile)),
        pltpu.SemaphoreType.DMA((3,)),
        pltpu.SemaphoreType.DMA((2, plane)),
    ]
    shapes = [like((height, width))] * plane + [like((rows, hid))] * 3
    shapes += [like((LINE * plane if last else plane, 128), F32)]
    specs = [hbm()] * (plane + 3) + [whole()]
    if last:
        scratch += [
            pltpu.VMEM((plane * EXTRA, width), BF16),
            pltpu.SemaphoreType.DMA((plane,)),
            pltpu.SemaphoreType.DMA((2,)),
        ]
        shapes += [like((plane * over, width))] * 2
        specs += [hbm()] * 2
    out = call(
        functools.partial(expert_kernel, plane, main, tile, last),
        [*ins, *weights, *earlier],
        [hbm()] * (plane + 3) + [whole()] * len(earlier),
        shapes,
        specs,
        after,
        10.0,
        scratch,
    )
    return out[:plane], out[plane : plane + 3], out[plane + 3], out[plane + 4 :]


def weight_kernel(plane, main, chunks, tailed, addends, half_ref, *refs):
    messages, refs = refs[: plane * chunks], refs[plane * chunks :]
    narrow = [refs[r * 3 : (r + 1) * 3] for r in range(chunks)]
    refs = refs[3 * chunks :]
    tails, refs = refs[:tailed], refs[tailed:]
    more, refs = refs[:addends], refs[addends:]
    scratch = refs[-7 - (2 if addends else 0) :]
    outs = refs[: len(refs) - len(scratch)]
    rows_x, rows_s, nbuf, obuf, m_sem, n_sem, out_sem = scratch[:7]
    units, width = obuf.shape[1:]
    first = pl.multiple_of(half_ref[0] * units, units)

    def load(i):
        copies, at = [], 0
        for r in range(chunks):
            size = narrow[r][i].shape[0]
            copies.append(
                pltpu.make_async_copy(
                    narrow[r][i].at[:, pl.ds(first, units)],
                    nbuf.at[i, pl.ds(at, size), :],
                    n_sem.at[i, r],
                )
            )
            at += size
        return copies

    def load_rows(i, target):
        copies, at = [], 0
        for k, message in enumerate(messages):
            copies.append(
                pltpu.make_async_copy(
                    message.at[pl.ds(i * main, main), :],
                    target.at[pl.ds(at, main), :],
                    m_sem.at[i, k],
                )
            )
            at += main
        if tailed:
            copies.append(
                pltpu.make_async_copy(
                    tails[i], target.at[pl.ds(at, tails[i].shape[0]), :], m_sem.at[i, len(messages)]
                )
            )
        return copies

    order = (1, 2, 0)
    loads = [load(1) + load_rows(0, rows_x), load(2), load(0) + load_rows(1, rows_s)]
    if addends:
        abuf, a_sem = scratch[7:]
        for k in range(addends):
            for place in range(3):
                source = more[k].at[place, pl.ds(first, units), :] if k == 0 else more[k].at[place]
                loads[place].append(
                    pltpu.make_async_copy(source, abuf.at[k, place], a_sem.at[k, place])
                )
    for copies in loads:
        for copy in copies:
            copy.start()
    stores = []
    step = min(width, 512)
    for place, i in enumerate(order):
        for copy in loads[place]:
            copy.wait()
        right = rows_s if i == 0 else rows_x
        for n in range(0, width, step):
            cut = slice(n, n + step)
            total = dot(nbuf[i], right[:, cut], ((0,), (0,)))
            for k in range(addends):
                total = total + abuf[k, place, :, cut].astype(F32)
            obuf[place, :, cut] = total.astype(BF16)
        target = outs[place].at[0] if len(outs) == 3 else outs[0].at[place]
        stores.append(pltpu.make_async_copy(obuf.at[place], target, out_sem.at[place]))
        stores[-1].start()
    for copy in stores:
        copy.wait()


def weight_grads(half, messages, narrow, tails, more, main, units, split, micros, after):
    plane, chunks = len(messages[0]), len(messages)
    rows = chunks * plane * main + (tails[0].shape[0] if tails else 0)
    width = messages[0][0].shape[1]
    shapes = [(1, units, width)] * 3 if split else [(3, units, width)]
    scratch = [
        pltpu.VMEM((rows, width), BF16),
        pltpu.VMEM((rows, width), BF16),
        pltpu.VMEM((3, rows, units), BF16),
        pltpu.VMEM((3, units, width), BF16),
        pltpu.SemaphoreType.DMA((2, chunks * plane + 1)),
        pltpu.SemaphoreType.DMA((3, chunks)),
        pltpu.SemaphoreType.DMA((3,)),
    ]
    if more:
        scratch += [
            pltpu.VMEM((len(more), 3, units, width), BF16),
            pltpu.SemaphoreType.DMA((len(more), 3)),
        ]
    given = [a for m in messages for a in m] + [a for n in narrow for a in n]
    given += [*tails, *more]
    return call(
        functools.partial(weight_kernel, plane, main, chunks, len(tails), len(more)),
        [half, *given],
        [smem()] + [hbm()] * len(given),
        [like(s) for s in shapes],
        [hbm()] * len(shapes),
        after,
        micros,
        scratch,
    )


def scatter_kernel(plane, main, r, added, last, place_ref, prob_ref, *refs):
    backs, refs = refs[:plane], refs[plane:]
    tails, refs = refs[:plane], refs[plane:]
    more_in, refs = refs[:added], refs[added:]
    if last:
        dlogits_ref, router_ref, refs = refs[0], refs[1], refs[2:]
    out_ref, rows_ref, more_ref, rank_ref, sems = refs
    copies = []
    for s in range(plane):
        copies.append(
            pltpu.make_async_copy(
                backs[s].at[pl.ds(0, main), :], rows_ref.at[pl.ds(s * main, main), :], sems.at[0, s]
            )
        )
        copies.append(
            pltpu.make_async_copy(
                tails[s].at[pl.ds(main, EXTRA), :],
                more_ref.at[pl.ds(s * EXTRA, EXTRA), :],
                sems.at[1, s],
            )
        )
    for copy in copies:
        copy.start()
    z, q = place_ref[0], place_ref[1]
    rank_ref[...] = rank_of(prob_ref[...])
    picks, more = [], []
    for s in range(plane):
        rank_row = rank_ref[pl.ds(z * plane + (q ^ s), 1), :]
        picks.append(slots(rank_row, main))
        more.append(extra_slots(rank_row, main, r, 0))
    for copy in copies:
        copy.wait()
    total = dot(jnp.concatenate(picks, axis=0).astype(BF16), rows_ref[...], ((0,), (0,)))
    total = total + dot(jnp.concatenate(more, axis=0).astype(BF16), more_ref[...], ((0,), (0,)))
    for ref in more_in:
        total = total + ref[...].astype(F32)
    if last:
        total = total + dot(dlogits_ref[...], router_ref[...], ((0,), (0,)))
    out_ref[...] = total.astype(BF16)


def scatter(place, prob, backs, tails, main, r, added, router, after):
    plane = len(backs)
    width = backs[0].shape[1]
    experts, count = prob.shape
    operands = [place, prob, *backs, *tails, *added, *router]
    return call(
        functools.partial(scatter_kernel, plane, main, r, len(added), len(router) > 0),
        operands,
        [smem(), whole()] + [hbm()] * (2 * plane) + [whole()] * (len(added) + len(router)),
        like((count, width)),
        whole(),
        after,
        2.5,
        [
            pltpu.VMEM((plane * main, width), BF16),
            pltpu.VMEM((plane * EXTRA, width), BF16),
            pltpu.VMEM((experts, count), F32),
            pltpu.SemaphoreType.DMA((2, plane)),
        ],
    )


def router_kernel(prob_ref, score_ref, x_ref, dlogits_ref, term_ref, dense_ref):
    prob = prob_ref[...]
    rank = rank_of(prob)
    member = prob >= 0.0
    score = score_ref[...]
    high = score.astype(BF16)
    rest = score - high.astype(F32)
    mid = rest.astype(BF16)
    low = (rest - mid.astype(F32)).astype(BF16)
    for e in range(prob.shape[0]):
        pick = slots(rank[e : e + 1, :], score.shape[1]).astype(BF16)
        value = dot(high[e : e + 1, :], pick, ((1,), (0,)))
        value = value + dot(mid[e : e + 1, :], pick, ((1,), (0,)))
        dense_ref[e : e + 1, :] = value + dot(low[e : e + 1, :], pick, ((1,), (0,)))
    weighted = dense_ref[...]
    both = weighted - prob * jnp.sum(weighted, axis=0, keepdims=True)
    dlogits = jnp.where(member, both, 0.0).astype(BF16)
    dlogits_ref[...] = dlogits
    term_ref[...] = dot(dlogits, x_ref[...], ((1,), (0,)))


def router_grads(prob, score, x):
    experts, count = prob.shape
    width = x.shape[1]
    return call(
        router_kernel,
        [prob, score, x],
        [whole()] * 3,
        [like((experts, count)), like((experts, width), F32)],
        [whole()] * 2,
        (),
        2.5,
        [pltpu.VMEM((experts, count), F32)],
    )


def local(tokens_in, grad_out, routes, router_weight, w_gate, w_up, w_down):
    count, width = tokens_in.shape
    experts = router_weight.shape[1]
    main = count * routes.shape[1] // experts
    plane = experts // LINE
    me = lax.axis_index("expert")
    z, q = me // plane, me % plane
    end = ((z == 0) | (z == LINE - 1)).astype(jnp.int32)
    place = jnp.stack([z, q, end]).astype(jnp.int32)
    router_t = router_weight.T

    def line(pairs):
        return [(a * plane + i, b * plane + i) for a, b in pairs for i in range(plane)]

    pair_swap = line([(0, 1), (1, 0), (2, 3), (3, 2)])
    mid_swap = line([(1, 2), (2, 1)])
    outward = line([(1, 0), (2, 3)])
    inward = line([(0, 1), (3, 2)])
    send = lambda a, perm: lax.ppermute(a, "expert", perm)
    across = lambda a, bit: send(a, [(i, i ^ bit) for i in range(experts)])

    prob, own = call(
        gate_kernel,
        [routes.T, tokens_in, grad_out, router_t],
        [whole()] * 4,
        [like((experts, count), F32), like((2 * count + group(experts), width))],
        [whole()] * 2,
        (),
        3.0,
    )
    near, mid = send(own, pair_swap), send(own, mid_swap)
    near2, mid2 = send(mid, outward), send(near, mid_swap)
    far = send(mid2, outward)
    cands = [(own,), (near,), (near2, mid2), (far, mid)]

    weights = (w_gate, w_up, w_down)
    messages, probs, parts, narrow, scores = [], [], [], [], []

    def pick_rows(r, tail, after):
        rows, block_prob, tail = compact(
            place, cands[r], tail, plane, experts, count, main, r, after
        )
        probs.append(block_prob)
        messages.append([rows[0]] + [across(rows[s], s) for s in range(1, plane)])
        return tail

    def run_expert(r, after):
        out = expert(messages[r], weights, main, scores if r == LINE - 1 else [], after)
        parts.append(out[0])
        narrow.append(out[1])
        scores.append(out[2])
        return out[3]

    tail = pick_rows(0, None, ())
    tail = pick_rows(1, tail, ())
    run_expert(0, (tail,))
    tail = pick_rows(2, tail, (scores[0],))
    run_expert(1, (tail,))
    tail = pick_rows(3, tail, (scores[1],))
    run_expert(2, (tail,))
    hid = w_gate.shape[1]
    units = hid // lax.axis_size("dp")
    half = lax.axis_index("dp").reshape(1).astype(jnp.int32)
    swap = [(i, 1 - i) for i in range(2)]
    (early,) = weight_grads(
        jnp.zeros_like(half), messages[: LINE - 1], narrow, (), (), main, hid, False, 11.0, ()
    )
    tails = run_expert(3, (early,))

    def tied(a, *others):
        return lax.optimization_barrier((a, *others))[0]

    back = [[parts[r][0]] + [across(parts[r][s], s) for s in range(1, plane)] for r in range(LINE)]
    join = lambda r, added, router, after: scatter(
        place, probs[r], back[r], back[-1], main, r, added, router, after
    )
    given = messages[-1:], narrow[-1:], tails
    (gone,) = weight_grads(1 - half, *given, (early,), main, units, False, 6.0, ())

    sum3 = join(3, [], (), (gone,))
    other = lax.ppermute(tied(gone, sum3), "dp", swap)
    packed = tied(scores[-1], sum3)[jnp.arange(experts) ^ me]
    score = lax.all_to_all(packed, "expert", split_axis=0, concat_axis=0, tiled=True)

    sum2 = join(2, [send(sum3, inward)], (), (score,))
    sum3 = (sum3.astype(F32) + send(sum2, inward).astype(F32)).astype(BF16)
    dlogits, term = router_grads(prob, tied(score, sum2), tokens_in)
    grads = weight_grads(half, *given, (early, other), main, units, True, 7.0, (sum2,))

    sum1 = join(1, [send(sum2, mid_swap)], (), (term, grads[0]))

    def tree(values):
        while len(values) > 1:
            values = [values[i] + values[i + 1] for i in range(0, len(values), 2)]
        return values[0]

    term = tied(term, sum1)
    term = tree([term] + [across(term, s) for s in range(1, plane)])
    term = tree([term] + [across(term, r * plane) for r in range(1, LINE)])
    term = term + lax.ppermute(term, "dp", swap)
    grad_router = term.T / count
    got = [send(sum1, pair_swap), send(sum3, mid_swap)]
    grad_x = join(0, got, (dlogits, router_t), (term,))
    return (grad_x, *grads, grad_router)


def solution(mesh):
    return jax.shard_map(
        local,
        mesh=mesh,
        in_specs=(
            P(("dp", "expert"), None),
            P(("dp", "expert"), None),
            P(("dp", "expert"), None),
            P(),
            P("expert", None, None),
            P("expert", None, None),
            P("expert", None, None),
        ),
        out_specs=(
            P(("dp", "expert"), None),
            P("expert", "dp", None),
            P("expert", "dp", None),
            P("expert", "dp", None),
            P(),
        ),
        check_vma=False,
    )
```

```python
import functools

import jax
import jax.numpy as jnp
from jax import lax
from jax.experimental import pallas as pl
from jax.experimental.pallas import tpu as pltpu
from jax.sharding import PartitionSpec as P

LINE = 4
OVER = 2
EXTRA = 16
MIB = 1 << 20
SPEED = 1.1e9
F32 = jnp.float32
BF16 = jnp.bfloat16


def dot(a, b, contract):
    return lax.dot_general(a, b, (contract, ((), ())), preferred_element_type=F32)


def hbm():
    return pl.BlockSpec(memory_space=pl.ANY)


def whole():
    return pl.BlockSpec(memory_space=pltpu.VMEM)


def smem():
    return pl.BlockSpec(memory_space=pltpu.SMEM)


def call(kernel, operands, in_specs, out_shape, out_specs, after, micros, scratch=(), limit=16):
    count, more = len(operands), len(after)

    def body(*refs):
        kernel(*refs[:count], *refs[count + more :])

    return pl.pallas_call(
        body,
        out_shape=out_shape,
        in_specs=list(in_specs) + [hbm()] * more,
        out_specs=out_specs,
        scratch_shapes=scratch,
        compiler_params=pltpu.CompilerParams(vmem_limit_bytes=limit * MIB),
        cost_estimate=pl.CostEstimate(
            flops=int(micros * SPEED), bytes_accessed=1024, transcendentals=0
        ),
    )(*operands, *after)


def like(shape, kind=BF16):
    return jax.ShapeDtypeStruct(shape, kind)


def group(size):
    return -(-size // 16) * 16


def gate_kernel(routes_ref, x_ref, g_ref, router_ref, prob_ref, out_ref):
    logits = dot(router_ref[...], x_ref[...], ((1,), (1,)))
    row = lax.broadcasted_iota(jnp.int32, logits.shape, 0)
    member = row == routes_ref[0:1, :]
    for k in range(1, routes_ref.shape[0]):
        member = member | (row == routes_ref[k : k + 1, :])
    top = jnp.max(jnp.where(member, logits, -jnp.inf), axis=0, keepdims=True)
    weight = jnp.where(member, jnp.exp(logits - top), 0.0)
    prob = jnp.where(member, weight / jnp.sum(weight, axis=0, keepdims=True), -1.0)
    prob_ref[...] = prob
    experts, count = prob.shape
    out_ref[0:count, :] = x_ref[...]
    out_ref[count : 2 * count, :] = g_ref[...]
    rest = prob
    for k in range(3):
        piece = rest.astype(BF16)
        rest = rest - piece.astype(F32)
        out_ref[2 * count : 2 * count + experts, k * count : (k + 1) * count] = piece
    tail = out_ref.shape[1] - 3 * count
    out_ref[2 * count : 2 * count + experts, 3 * count :] = jnp.zeros((experts, tail), BF16)


def rank_of(prob):
    count = prob.shape[1]
    earlier = lax.broadcasted_iota(jnp.int32, (count, count), 0) < lax.broadcasted_iota(
        jnp.int32, (count, count), 1
    )
    member = prob >= 0.0
    rank = dot(member.astype(F32).astype(BF16), earlier.astype(F32).astype(BF16), ((1,), (0,)))
    return jnp.where(member, rank, -1.0)


def slots(rank_row, count):
    row = lax.broadcasted_iota(jnp.int32, (count, rank_row.shape[1]), 0).astype(F32)
    return (row == rank_row).astype(F32)


def extra_slots(rank_row, main, r, shift):
    row = lax.broadcasted_iota(jnp.int32, (EXTRA, rank_row.shape[1]), 0).astype(F32)
    row = row - float(shift + OVER * r)
    return ((row >= 0.0) & (row < OVER) & (row + main == rank_row)).astype(F32)


def compact_kernel(plane, main, r, cands, place_ref, *refs):
    z, q, end = place_ref[0], place_ref[1], place_ref[2]
    given, refs = refs[:cands], refs[cands:]
    if r > 0:
        tail_in, refs = refs[0], refs[1:]
    outs, refs = refs[:plane], refs[plane:]
    prob_ref, tail_ref, rank_ref = refs
    experts, count = prob_ref.shape
    block = given[0][...]
    if cands == 2:
        block = jnp.where(end > 0, block, given[1][...])
    rows_x, rows_s = block[0:count], block[count : 2 * count]
    pieces = [
        block[2 * count : 2 * count + experts, k * count : (k + 1) * count].astype(F32)
        for k in range(3)
    ]
    prob_ref[...] = (pieces[0] + pieces[1]) + pieces[2]
    rank_ref[...] = rank_of(prob_ref[...])
    picks, more_x, more_s, factor, more_factor = [], [], [], [], []
    for s in range(plane):
        expert = z * plane + (q ^ s)
        rank_row = rank_ref[pl.ds(expert, 1), :]
        prob_row = prob_ref[pl.ds(expert, 1), :]
        picks.append(slots(rank_row, main))
        more_x.append(extra_slots(rank_row, main, r, 0))
        more_s.append(extra_slots(rank_row, main, r, LINE * OVER))
        factor.append(jnp.sum(picks[-1] * prob_row, axis=1, keepdims=True))
        more_factor.append(jnp.sum(more_s[-1] * prob_row, axis=1, keepdims=True))
    pick = jnp.concatenate(picks, axis=0).astype(BF16)
    value_x = dot(pick, rows_x, ((1,), (0,)))
    value_s = dot(pick, rows_s, ((1,), (0,))) * jnp.concatenate(factor, axis=0)
    tail = dot(jnp.concatenate(more_x, axis=0).astype(BF16), rows_x, ((1,), (0,)))
    tail_s = dot(jnp.concatenate(more_s, axis=0).astype(BF16), rows_s, ((1,), (0,)))
    tail = tail + tail_s * jnp.concatenate(more_factor, axis=0)
    if r > 0:
        tail = tail + tail_in[...].astype(F32)
    tail_ref[...] = tail.astype(BF16)
    for s in range(plane):
        part = slice(s * main, (s + 1) * main)
        outs[s][0:main, :] = value_x[part].astype(BF16)
        outs[s][main : 2 * main, :] = value_s[part].astype(BF16)
        if r == LINE - 1:
            outs[s][2 * main :, :] = tail[s * EXTRA : (s + 1) * EXTRA].astype(BF16)


def compact(place, cands, tail, plane, experts, count, main, r, after):
    width = cands[0].shape[1]
    height = 2 * main + (EXTRA if r == LINE - 1 else 0)
    operands = [place, *cands] + ([] if tail is None else [tail])
    out = call(
        functools.partial(compact_kernel, plane, main, r, len(cands)),
        operands,
        [smem()] + [whole()] * (len(operands) - 1),
        [like((height, width))] * plane
        + [like((experts, count), F32), like((plane * EXTRA, width))],
        [whole()] * (plane + 2),
        after,
        3.0,
        [pltpu.VMEM((experts, count), F32)],
    )
    return out[:plane], out[plane], out[plane + 1]


def expert_kernel(plane, main, tile, last, *refs):
    ins, weights, refs = refs[:plane], refs[plane : plane + 3], refs[plane + 3 :]
    if last:
        earlier, refs = refs[: LINE - 1], refs[LINE - 1 :]
    parts, narrow, score_ref = refs[:plane], refs[plane : plane + 3], refs[plane + 3]
    refs = refs[plane + 4 :]
    if last:
        tails, refs = refs[:2], refs[2:]
        ebuf, e_sem, t_sem = refs[-3:]
    rows_x, rows_s, wbuf, nbuf, pbuf, row_sem, w_sem, n_sem, p_sem = refs[:9]
    hid, width = wbuf.shape[1:]
    tiles = hid // tile
    base = plane * main
    over = LINE * OVER

    row_copies = []
    for s in range(plane):
        own = pl.ds(s * main, main)
        for i, target in enumerate((rows_x, rows_s)):
            row_copies.append(
                pltpu.make_async_copy(
                    ins[s].at[pl.ds(i * main, main), :], target.at[own, :], row_sem.at[i, s]
                )
            )
        if last:
            row_copies.append(
                pltpu.make_async_copy(
                    ins[s].at[pl.ds(2 * main, EXTRA), :],
                    ebuf.at[pl.ds(s * EXTRA, EXTRA), :],
                    e_sem.at[s],
                )
            )
    w_copies = [
        [
            pltpu.make_async_copy(
                weights[i].at[0, pl.ds(f * tile, tile), :],
                wbuf.at[i, pl.ds(f * tile, tile), :],
                w_sem.at[i, f],
            )
            for i in range(3)
        ]
        for f in range(tiles)
    ]
    for copy in row_copies:
        copy.start()
    for part in w_copies:
        for copy in part:
            copy.start()
    for copy in row_copies:
        copy.wait()
    stores = []
    if last:
        extra = ebuf[...].astype(F32)
        first = [extra[s * EXTRA : s * EXTRA + over] for s in range(plane)]
        second = [extra[s * EXTRA + over : s * EXTRA + 2 * over] for s in range(plane)]
        rows_x[base:, :] = jnp.concatenate(first, axis=0).astype(BF16)
        rows_s[base:, :] = jnp.concatenate(second, axis=0).astype(BF16)
        for i, source in enumerate((rows_x, rows_s)):
            stores.append(
                pltpu.make_async_copy(
                    source.at[pl.ds(base, plane * over), :], tails[i], t_sem.at[i]
                )
            )
            stores[-1].start()

    score = jnp.zeros((rows_x.shape[0], 1), F32)
    for f in range(tiles):
        cut = slice(f * tile, (f + 1) * tile)
        for copy in w_copies[f]:
            copy.wait()
        pre_gate = dot(rows_x[...], wbuf[0, cut, :], ((1,), (1,)))
        pre_up = dot(rows_x[...], wbuf[1, cut, :], ((1,), (1,)))
        grad_hidden = dot(rows_s[...], wbuf[2, cut, :], ((1,), (1,)))
        sig = jax.nn.sigmoid(pre_gate)
        act = pre_gate * sig
        hidden = (act * pre_up).astype(BF16)
        nbuf[0, :, cut] = hidden
        nbuf[1, :, cut] = (grad_hidden * pre_up * sig * (1.0 + pre_gate * (1.0 - sig))).astype(BF16)
        nbuf[2, :, cut] = (grad_hidden * act).astype(BF16)
        score = score + jnp.sum(hidden.astype(F32) * grad_hidden, axis=1, keepdims=True)
    for i in range(3):
        stores.append(pltpu.make_async_copy(nbuf.at[i], narrow[i], n_sem.at[i]))
        stores[-1].start()
    step = min(width, 512)
    for n in range(0, width, step):
        cut = slice(n, n + step)
        total = dot(nbuf[1], wbuf[0, :, cut], ((1,), (0,)))
        total = total + dot(nbuf[2], wbuf[1, :, cut], ((1,), (0,)))
        pbuf[0:base, cut] = total[0:base].astype(BF16)
        if last:
            blank = jnp.zeros((EXTRA - over, step), F32)
            for s in range(plane):
                more = total[base + s * over : base + (s + 1) * over]
                more = jnp.concatenate([more, blank], axis=0).astype(BF16)
                pbuf[base + s * EXTRA : base + (s + 1) * EXTRA, cut] = more
    for s in range(plane):
        stores.append(
            pltpu.make_async_copy(
                pbuf.at[pl.ds(s * main, main), :],
                parts[s].at[pl.ds(0, main), :],
                p_sem.at[0, s],
            )
        )
        stores[-1].start()
        if last:
            stores.append(
                pltpu.make_async_copy(
                    pbuf.at[pl.ds(base + s * EXTRA, EXTRA), :],
                    parts[s].at[pl.ds(main, EXTRA), :],
                    p_sem.at[1, s],
                )
            )
            stores[-1].start()

    def lanes(column, shift, width=128):
        shape = (column.shape[0], width)
        row = lax.broadcasted_iota(jnp.int32, shape, 0) + shift
        lane = lax.broadcasted_iota(jnp.int32, shape, 1)
        return jnp.sum(jnp.where(row == lane, column, 0.0), axis=0, keepdims=True)

    own = [lanes(score[s * main : (s + 1) * main], 0) for s in range(plane)]
    if not last:
        score_ref[...] = jnp.concatenate(own, axis=0)
    else:
        lane = lax.broadcasted_iota(jnp.int32, (1, 128), 1)
        over_rows = [
            lanes(score[base + s * over : base + (s + 1) * over], main) for s in range(plane)
        ]
        for r in range(LINE):
            for s in range(plane):
                value = own[s] if r == LINE - 1 else earlier[r][s : s + 1, :]
                for j in range(OVER):
                    at = main + OVER * r + j
                    one = jnp.sum(jnp.where(lane == at, over_rows[s], 0.0), axis=1, keepdims=True)
                    value = jnp.where(lane == main + j, one, value)
                score_ref[r * plane + s : r * plane + s + 1, :] = value
    for copy in stores:
        copy.wait()


def expert(ins, weights, main, earlier, after):
    plane = len(ins)
    width = ins[0].shape[1]
    last = len(earlier) > 0
    hid = weights[0].shape[1]
    base, over = plane * main, LINE * OVER
    rows = base + (plane * over if last else 0)
    spread = base + (plane * EXTRA if last else 0)
    tile = 256 if hid % 256 == 0 else hid
    height = main + (EXTRA if last else 0)
    scratch = [
        pltpu.VMEM((rows, width), BF16),
        pltpu.VMEM((rows, width), BF16),
        pltpu.VMEM((3, hid, width), BF16),
        pltpu.VMEM((3, rows, hid), BF16),
        pltpu.VMEM((spread, width), BF16),
        pltpu.SemaphoreType.DMA((2, plane)),
        pltpu.SemaphoreType.DMA((3, hid // tile)),
        pltpu.SemaphoreType.DMA((3,)),
        pltpu.SemaphoreType.DMA((2, plane)),
    ]
    shapes = [like((height, width))] * plane + [like((rows, hid))] * 3
    shapes += [like((LINE * plane if last else plane, 128), F32)]
    specs = [hbm()] * (plane + 3) + [whole()]
    if last:
        scratch += [
            pltpu.VMEM((plane * EXTRA, width), BF16),
            pltpu.SemaphoreType.DMA((plane,)),
            pltpu.SemaphoreType.DMA((2,)),
        ]
        shapes += [like((plane * over, width))] * 2
        specs += [hbm()] * 2
    out = call(
        functools.partial(expert_kernel, plane, main, tile, last),
        [*ins, *weights, *earlier],
        [hbm()] * (plane + 3) + [whole()] * len(earlier),
        shapes,
        specs,
        after,
        10.0,
        scratch,
        60 if last else 32,
    )
    return out[:plane], out[plane : plane + 3], out[plane + 3], out[plane + 4 :]


def weight_kernel(plane, main, chunks, tailed, addends, half_ref, *refs):
    messages, refs = refs[: plane * chunks], refs[plane * chunks :]
    narrow = [refs[r * 3 : (r + 1) * 3] for r in range(chunks)]
    refs = refs[3 * chunks :]
    tails, refs = refs[:tailed], refs[tailed:]
    more, refs = refs[:addends], refs[addends:]
    scratch = refs[-7 - (2 if addends else 0) :]
    outs = refs[: len(refs) - len(scratch)]
    rows_x, rows_s, nbuf, obuf, m_sem, n_sem, out_sem = scratch[:7]
    units, width = obuf.shape[1:]
    first = pl.multiple_of(half_ref[0] * units, units)

    def load(i):
        copies, at = [], 0
        for r in range(chunks):
            size = narrow[r][i].shape[0]
            copies.append(
                pltpu.make_async_copy(
                    narrow[r][i].at[:, pl.ds(first, units)],
                    nbuf.at[i, pl.ds(at, size), :],
                    n_sem.at[i, r],
                )
            )
            at += size
        return copies

    def load_rows(i, target):
        copies, at = [], 0
        for k, message in enumerate(messages):
            copies.append(
                pltpu.make_async_copy(
                    message.at[pl.ds(i * main, main), :],
                    target.at[pl.ds(at, main), :],
                    m_sem.at[i, k],
                )
            )
            at += main
        if tailed:
            copies.append(
                pltpu.make_async_copy(
                    tails[i], target.at[pl.ds(at, tails[i].shape[0]), :], m_sem.at[i, len(messages)]
                )
            )
        return copies

    order = (1, 2, 0)
    loads = [load(1) + load_rows(0, rows_x), load(2), load(0) + load_rows(1, rows_s)]
    if addends:
        abuf, a_sem = scratch[7:]
        for k in range(addends):
            for place in range(3):
                source = more[k].at[place, pl.ds(first, units), :] if k == 0 else more[k].at[place]
                loads[place].append(
                    pltpu.make_async_copy(source, abuf.at[k, place], a_sem.at[k, place])
                )
    for copies in loads:
        for copy in copies:
            copy.start()
    stores = []
    step = min(width, 512)
    for place, i in enumerate(order):
        for copy in loads[place]:
            copy.wait()
        right = rows_s if i == 0 else rows_x
        for n in range(0, width, step):
            cut = slice(n, n + step)
            total = dot(nbuf[i], right[:, cut], ((0,), (0,)))
            for k in range(addends):
                total = total + abuf[k, place, :, cut].astype(F32)
            obuf[place, :, cut] = total.astype(BF16)
        target = outs[place].at[0] if len(outs) == 3 else outs[0].at[place]
        stores.append(pltpu.make_async_copy(obuf.at[place], target, out_sem.at[place]))
        stores[-1].start()
    for copy in stores:
        copy.wait()


def weight_grads(half, messages, narrow, tails, more, main, units, split, micros, after):
    plane, chunks = len(messages[0]), len(messages)
    rows = chunks * plane * main + (tails[0].shape[0] if tails else 0)
    width = messages[0][0].shape[1]
    shapes = [(1, units, width)] * 3 if split else [(3, units, width)]
    scratch = [
        pltpu.VMEM((rows, width), BF16),
        pltpu.VMEM((rows, width), BF16),
        pltpu.VMEM((3, rows, units), BF16),
        pltpu.VMEM((3, units, width), BF16),
        pltpu.SemaphoreType.DMA((2, chunks * plane + 1)),
        pltpu.SemaphoreType.DMA((3, chunks)),
        pltpu.SemaphoreType.DMA((3,)),
    ]
    if more:
        scratch += [
            pltpu.VMEM((len(more), 3, units, width), BF16),
            pltpu.SemaphoreType.DMA((len(more), 3)),
        ]
    given = [a for m in messages for a in m] + [a for n in narrow for a in n]
    given += [*tails, *more]
    return call(
        functools.partial(weight_kernel, plane, main, chunks, len(tails), len(more)),
        [half, *given],
        [smem()] + [hbm()] * len(given),
        [like(s) for s in shapes],
        [hbm()] * len(shapes),
        after,
        micros,
        scratch,
        60 if more else 50,
    )


def scatter_kernel(plane, main, r, added, last, place_ref, prob_ref, *refs):
    backs, refs = refs[:plane], refs[plane:]
    tails, refs = refs[:plane], refs[plane:]
    more_in, refs = refs[:added], refs[added:]
    if last:
        dlogits_ref, router_ref, refs = refs[0], refs[1], refs[2:]
    out_ref, rows_ref, more_ref, rank_ref, sems = refs
    copies = []
    for s in range(plane):
        copies.append(
            pltpu.make_async_copy(
                backs[s].at[pl.ds(0, main), :], rows_ref.at[pl.ds(s * main, main), :], sems.at[0, s]
            )
        )
        copies.append(
            pltpu.make_async_copy(
                tails[s].at[pl.ds(main, EXTRA), :],
                more_ref.at[pl.ds(s * EXTRA, EXTRA), :],
                sems.at[1, s],
            )
        )
    for copy in copies:
        copy.start()
    z, q = place_ref[0], place_ref[1]
    rank_ref[...] = rank_of(prob_ref[...])
    picks, more = [], []
    for s in range(plane):
        rank_row = rank_ref[pl.ds(z * plane + (q ^ s), 1), :]
        picks.append(slots(rank_row, main))
        more.append(extra_slots(rank_row, main, r, 0))
    for copy in copies:
        copy.wait()
    total = dot(jnp.concatenate(picks, axis=0).astype(BF16), rows_ref[...], ((0,), (0,)))
    total = total + dot(jnp.concatenate(more, axis=0).astype(BF16), more_ref[...], ((0,), (0,)))
    for ref in more_in:
        total = total + ref[...].astype(F32)
    if last:
        total = total + dot(dlogits_ref[...], router_ref[...], ((0,), (0,)))
    out_ref[...] = total.astype(BF16)


def scatter(place, prob, backs, tails, main, r, added, router, after):
    plane = len(backs)
    width = backs[0].shape[1]
    experts, count = prob.shape
    operands = [place, prob, *backs, *tails, *added, *router]
    return call(
        functools.partial(scatter_kernel, plane, main, r, len(added), len(router) > 0),
        operands,
        [smem(), whole()] + [hbm()] * (2 * plane) + [whole()] * (len(added) + len(router)),
        like((count, width)),
        whole(),
        after,
        0.02,
        [
            pltpu.VMEM((plane * main, width), BF16),
            pltpu.VMEM((plane * EXTRA, width), BF16),
            pltpu.VMEM((experts, count), F32),
            pltpu.SemaphoreType.DMA((2, plane)),
        ],
    )


def router_kernel(prob_ref, score_ref, x_ref, dlogits_ref, term_ref, dense_ref):
    prob = prob_ref[...]
    rank = rank_of(prob)
    member = prob >= 0.0
    score = score_ref[...]
    high = score.astype(BF16)
    rest = score - high.astype(F32)
    mid = rest.astype(BF16)
    low = (rest - mid.astype(F32)).astype(BF16)
    for e in range(prob.shape[0]):
        pick = slots(rank[e : e + 1, :], score.shape[1]).astype(BF16)
        value = dot(high[e : e + 1, :], pick, ((1,), (0,)))
        value = value + dot(mid[e : e + 1, :], pick, ((1,), (0,)))
        dense_ref[e : e + 1, :] = value + dot(low[e : e + 1, :], pick, ((1,), (0,)))
    weighted = dense_ref[...]
    both = weighted - prob * jnp.sum(weighted, axis=0, keepdims=True)
    dlogits = jnp.where(member, both, 0.0).astype(BF16)
    dlogits_ref[...] = dlogits
    term_ref[...] = dot(dlogits, x_ref[...], ((1,), (0,)))


def router_grads(prob, score, x):
    experts, count = prob.shape
    width = x.shape[1]
    return call(
        router_kernel,
        [prob, score, x],
        [whole()] * 3,
        [like((experts, count)), like((experts, width), F32)],
        [whole()] * 2,
        (),
        0.02,
        [pltpu.VMEM((experts, count), F32)],
    )


def local(tokens_in, grad_out, routes, router_weight, w_gate, w_up, w_down):
    count, width = tokens_in.shape
    experts = router_weight.shape[1]
    main = count * routes.shape[1] // experts
    plane = experts // LINE
    me = lax.axis_index("expert")
    z, q = me // plane, me % plane
    end = ((z == 0) | (z == LINE - 1)).astype(jnp.int32)
    place = jnp.stack([z, q, end]).astype(jnp.int32)
    router_t = router_weight.T

    def line(pairs):
        return [(a * plane + i, b * plane + i) for a, b in pairs for i in range(plane)]

    pair_swap = line([(0, 1), (1, 0), (2, 3), (3, 2)])
    mid_swap = line([(1, 2), (2, 1)])
    outward = line([(1, 0), (2, 3)])
    inward = line([(0, 1), (3, 2)])
    send = lambda a, perm: lax.ppermute(a, "expert", perm)
    across = lambda a, bit: send(a, [(i, i ^ bit) for i in range(experts)])

    prob, own = call(
        gate_kernel,
        [routes.T, tokens_in, grad_out, router_t],
        [whole()] * 4,
        [like((experts, count), F32), like((2 * count + group(experts), width))],
        [whole()] * 2,
        (),
        3.0,
    )
    near, mid = send(own, pair_swap), send(own, mid_swap)
    near2, mid2 = send(mid, outward), send(near, mid_swap)
    far = send(mid2, outward)
    cands = [(own,), (near,), (near2, mid2), (far, mid)]

    weights = (w_gate, w_up, w_down)
    messages, probs, parts, narrow, scores = [], [], [], [], []

    def pick_rows(r, tail, after):
        rows, block_prob, tail = compact(
            place, cands[r], tail, plane, experts, count, main, r, after
        )
        probs.append(block_prob)
        messages.append([rows[0]] + [across(rows[s], s) for s in range(1, plane)])
        return tail

    def run_expert(r, after):
        out = expert(messages[r], weights, main, scores if r == LINE - 1 else [], after)
        parts.append(out[0])
        narrow.append(out[1])
        scores.append(out[2])
        return out[3]

    tail = pick_rows(0, None, ())
    tail = pick_rows(1, tail, ())
    run_expert(0, (tail,))
    tail = pick_rows(2, tail, (scores[0],))
    run_expert(1, (tail,))
    tail = pick_rows(3, tail, (scores[1],))
    run_expert(2, (tail,))
    hid = w_gate.shape[1]
    units = hid // lax.axis_size("dp")
    half = lax.axis_index("dp").reshape(1).astype(jnp.int32)
    swap = [(i, 1 - i) for i in range(2)]
    (early,) = weight_grads(
        jnp.zeros_like(half), messages[: LINE - 1], narrow, (), (), main, hid, False, 11.0, ()
    )
    tails = run_expert(3, (early,))

    def tied(a, *others):
        return lax.optimization_barrier((a, *others))[0]

    back = [[parts[r][0]] + [across(parts[r][s], s) for s in range(1, plane)] for r in range(LINE)]
    join = lambda r, added, router, after: scatter(
        place, probs[r], back[r], back[-1], main, r, added, router, after
    )
    given = messages[-1:], narrow[-1:], tails
    (gone,) = weight_grads(1 - half, *given, (early,), main, units, False, 0.05, ())

    sum3 = join(3, [], (), (gone,))
    other = lax.ppermute(tied(gone, sum3), "dp", swap)
    packed = tied(scores[-1], sum3)[jnp.arange(experts) ^ me]
    score = lax.all_to_all(packed, "expert", split_axis=0, concat_axis=0, tiled=True)

    sum2 = join(2, [send(sum3, inward)], (), (score,))
    sum3 = (sum3.astype(F32) + send(sum2, inward).astype(F32)).astype(BF16)
    dlogits, term = router_grads(prob, tied(score, sum2), tokens_in)

    def tree(values):
        while len(values) > 1:
            values = [values[i] + values[i + 1] for i in range(0, len(values), 2)]
        return values[0]

    term = tree([term] + [across(term, s) for s in range(1, plane)])
    sum1 = join(1, [send(sum2, mid_swap)], (), (term,))
    grads = weight_grads(half, *given, (early, other), main, units, True, 0.05, (sum1,))
    got = [send(sum1, pair_swap), send(sum3, mid_swap)]
    grad_x = join(0, got, (dlogits, router_t), (grads[0],))
    term = tied(term, grads[0])
    term = tree([term] + [across(term, r * plane) for r in range(1, LINE)])
    term = tied(term, grad_x)
    term = term + lax.ppermute(term, "dp", swap)
    grad_router = term.T / count
    return (grad_x, *grads, grad_router)


def solution(mesh):
    return jax.shard_map(
        local,
        mesh=mesh,
        in_specs=(
            P(("dp", "expert"), None),
            P(("dp", "expert"), None),
            P(("dp", "expert"), None),
            P(),
            P("expert", None, None),
            P("expert", None, None),
            P("expert", None, None),
        ),
        out_specs=(
            P(("dp", "expert"), None),
            P("expert", "dp", None),
            P("expert", "dp", None),
            P("expert", "dp", None),
            P(),
        ),
        check_vma=False,
    )
```

```python
import functools

import jax
import jax.numpy as jnp
from jax import lax
from jax.experimental import pallas as pl
from jax.experimental.pallas import tpu as pltpu
from jax.sharding import PartitionSpec as P

LINE = 4
OVER = 2
EXTRA = 16
MIB = 1 << 20
SPEED = 1.1e9
F32 = jnp.float32
BF16 = jnp.bfloat16


def dot(a, b, contract):
    return lax.dot_general(a, b, (contract, ((), ())), preferred_element_type=F32)


def hbm():
    return pl.BlockSpec(memory_space=pl.ANY)


def whole():
    return pl.BlockSpec(memory_space=pltpu.VMEM)


def smem():
    return pl.BlockSpec(memory_space=pltpu.SMEM)


def call(kernel, operands, in_specs, out_shape, out_specs, after, micros, scratch=(), limit=16):
    count, more = len(operands), len(after)

    def body(*refs):
        kernel(*refs[:count], *refs[count + more :])

    return pl.pallas_call(
        body,
        out_shape=out_shape,
        in_specs=list(in_specs) + [hbm()] * more,
        out_specs=out_specs,
        scratch_shapes=scratch,
        compiler_params=pltpu.CompilerParams(vmem_limit_bytes=limit * MIB),
        cost_estimate=pl.CostEstimate(
            flops=int(micros * SPEED), bytes_accessed=1024, transcendentals=0
        ),
    )(*operands, *after)


def like(shape, kind=BF16):
    return jax.ShapeDtypeStruct(shape, kind)


def group(size):
    return -(-size // 16) * 16


def gate_kernel(routes_ref, x_ref, g_ref, router_ref, prob_ref, out_ref):
    logits = dot(router_ref[...], x_ref[...], ((1,), (1,)))
    row = lax.broadcasted_iota(jnp.int32, logits.shape, 0)
    member = row == routes_ref[0:1, :]
    for k in range(1, routes_ref.shape[0]):
        member = member | (row == routes_ref[k : k + 1, :])
    top = jnp.max(jnp.where(member, logits, -jnp.inf), axis=0, keepdims=True)
    weight = jnp.where(member, jnp.exp(logits - top), 0.0)
    prob = jnp.where(member, weight / jnp.sum(weight, axis=0, keepdims=True), -1.0)
    prob_ref[...] = prob
    experts, count = prob.shape
    out_ref[0:count, :] = x_ref[...]
    out_ref[count : 2 * count, :] = g_ref[...]
    rest = prob
    for k in range(3):
        piece = rest.astype(BF16)
        rest = rest - piece.astype(F32)
        out_ref[2 * count : 2 * count + experts, k * count : (k + 1) * count] = piece
    tail = out_ref.shape[1] - 3 * count
    out_ref[2 * count : 2 * count + experts, 3 * count :] = jnp.zeros((experts, tail), BF16)


def rank_of(prob):
    count = prob.shape[1]
    earlier = lax.broadcasted_iota(jnp.int32, (count, count), 0) < lax.broadcasted_iota(
        jnp.int32, (count, count), 1
    )
    member = prob >= 0.0
    rank = dot(member.astype(F32).astype(BF16), earlier.astype(F32).astype(BF16), ((1,), (0,)))
    return jnp.where(member, rank, -1.0)


def slots(rank_row, count):
    row = lax.broadcasted_iota(jnp.int32, (count, rank_row.shape[1]), 0).astype(F32)
    return (row == rank_row).astype(F32)


def extra_slots(rank_row, main, r, shift):
    row = lax.broadcasted_iota(jnp.int32, (EXTRA, rank_row.shape[1]), 0).astype(F32)
    row = row - float(shift + OVER * r)
    return ((row >= 0.0) & (row < OVER) & (row + main == rank_row)).astype(F32)


def compact_kernel(plane, main, r, cands, place_ref, *refs):
    z, q, end = place_ref[0], place_ref[1], place_ref[2]
    given, refs = refs[:cands], refs[cands:]
    if r > 0:
        tail_in, refs = refs[0], refs[1:]
    outs, refs = refs[:plane], refs[plane:]
    prob_ref, tail_ref, rank_ref = refs
    experts, count = prob_ref.shape
    block = given[0][...]
    if cands == 2:
        block = jnp.where(end > 0, block, given[1][...])
    rows_x, rows_s = block[0:count], block[count : 2 * count]
    pieces = [
        block[2 * count : 2 * count + experts, k * count : (k + 1) * count].astype(F32)
        for k in range(3)
    ]
    prob_ref[...] = (pieces[0] + pieces[1]) + pieces[2]
    rank_ref[...] = rank_of(prob_ref[...])
    picks, more_x, more_s, factor, more_factor = [], [], [], [], []
    for s in range(plane):
        expert = z * plane + (q ^ s)
        rank_row = rank_ref[pl.ds(expert, 1), :]
        prob_row = prob_ref[pl.ds(expert, 1), :]
        picks.append(slots(rank_row, main))
        more_x.append(extra_slots(rank_row, main, r, 0))
        more_s.append(extra_slots(rank_row, main, r, LINE * OVER))
        factor.append(jnp.sum(picks[-1] * prob_row, axis=1, keepdims=True))
        more_factor.append(jnp.sum(more_s[-1] * prob_row, axis=1, keepdims=True))
    pick = jnp.concatenate(picks, axis=0).astype(BF16)
    value_x = dot(pick, rows_x, ((1,), (0,)))
    value_s = dot(pick, rows_s, ((1,), (0,))) * jnp.concatenate(factor, axis=0)
    tail = dot(jnp.concatenate(more_x, axis=0).astype(BF16), rows_x, ((1,), (0,)))
    tail_s = dot(jnp.concatenate(more_s, axis=0).astype(BF16), rows_s, ((1,), (0,)))
    tail = tail + tail_s * jnp.concatenate(more_factor, axis=0)
    if r > 0:
        tail = tail + tail_in[...].astype(F32)
    tail_ref[...] = tail.astype(BF16)
    for s in range(plane):
        part = slice(s * main, (s + 1) * main)
        outs[s][0:main, :] = value_x[part].astype(BF16)
        outs[s][main : 2 * main, :] = value_s[part].astype(BF16)
        if r == LINE - 1:
            outs[s][2 * main :, :] = tail[s * EXTRA : (s + 1) * EXTRA].astype(BF16)


def compact(place, cands, tail, plane, experts, count, main, r, after):
    width = cands[0].shape[1]
    height = 2 * main + (EXTRA if r == LINE - 1 else 0)
    operands = [place, *cands] + ([] if tail is None else [tail])
    out = call(
        functools.partial(compact_kernel, plane, main, r, len(cands)),
        operands,
        [smem()] + [whole()] * (len(operands) - 1),
        [like((height, width))] * plane
        + [like((experts, count), F32), like((plane * EXTRA, width))],
        [whole()] * (plane + 2),
        after,
        3.0,
        [pltpu.VMEM((experts, count), F32)],
    )
    return out[:plane], out[plane], out[plane + 1]


def expert_kernel(plane, main, tile, last, *refs):
    ins, weights, refs = refs[:plane], refs[plane : plane + 3], refs[plane + 3 :]
    if last:
        earlier, refs = refs[: LINE - 1], refs[LINE - 1 :]
    parts, narrow, score_ref = refs[:plane], refs[plane : plane + 3], refs[plane + 3]
    refs = refs[plane + 4 :]
    if last:
        tails, refs = refs[:2], refs[2:]
        ebuf, e_sem, t_sem = refs[-3:]
    rows_x, rows_s, wbuf, nbuf, pbuf, row_sem, w_sem, n_sem, p_sem = refs[:9]
    hid, width = wbuf.shape[1:]
    tiles = hid // tile
    base = plane * main
    over = LINE * OVER

    row_copies = []
    for s in range(plane):
        own = pl.ds(s * main, main)
        for i, target in enumerate((rows_x, rows_s)):
            row_copies.append(
                pltpu.make_async_copy(
                    ins[s].at[pl.ds(i * main, main), :], target.at[own, :], row_sem.at[i, s]
                )
            )
        if last:
            row_copies.append(
                pltpu.make_async_copy(
                    ins[s].at[pl.ds(2 * main, EXTRA), :],
                    ebuf.at[pl.ds(s * EXTRA, EXTRA), :],
                    e_sem.at[s],
                )
            )
    w_copies = [
        [
            pltpu.make_async_copy(
                weights[i].at[0, pl.ds(f * tile, tile), :],
                wbuf.at[i, pl.ds(f * tile, tile), :],
                w_sem.at[i, f],
            )
            for i in range(3)
        ]
        for f in range(tiles)
    ]
    for copy in row_copies:
        copy.start()
    for part in w_copies:
        for copy in part:
            copy.start()
    for copy in row_copies:
        copy.wait()
    stores = []
    if last:
        extra = ebuf[...].astype(F32)
        first = [extra[s * EXTRA : s * EXTRA + over] for s in range(plane)]
        second = [extra[s * EXTRA + over : s * EXTRA + 2 * over] for s in range(plane)]
        rows_x[base:, :] = jnp.concatenate(first, axis=0).astype(BF16)
        rows_s[base:, :] = jnp.concatenate(second, axis=0).astype(BF16)
        for i, source in enumerate((rows_x, rows_s)):
            stores.append(
                pltpu.make_async_copy(
                    source.at[pl.ds(base, plane * over), :], tails[i], t_sem.at[i]
                )
            )
            stores[-1].start()

    score = jnp.zeros((rows_x.shape[0], 1), F32)
    for f in range(tiles):
        cut = slice(f * tile, (f + 1) * tile)
        for copy in w_copies[f]:
            copy.wait()
        pre_gate = dot(rows_x[...], wbuf[0, cut, :], ((1,), (1,)))
        pre_up = dot(rows_x[...], wbuf[1, cut, :], ((1,), (1,)))
        grad_hidden = dot(rows_s[...], wbuf[2, cut, :], ((1,), (1,)))
        sig = jax.nn.sigmoid(pre_gate)
        act = pre_gate * sig
        hidden = (act * pre_up).astype(BF16)
        nbuf[0, :, cut] = hidden
        nbuf[1, :, cut] = (grad_hidden * pre_up * sig * (1.0 + pre_gate * (1.0 - sig))).astype(BF16)
        nbuf[2, :, cut] = (grad_hidden * act).astype(BF16)
        score = score + jnp.sum(hidden.astype(F32) * grad_hidden, axis=1, keepdims=True)
    for i in range(3):
        stores.append(pltpu.make_async_copy(nbuf.at[i], narrow[i], n_sem.at[i]))
        stores[-1].start()
    step = min(width, 512)
    for n in range(0, width, step):
        cut = slice(n, n + step)
        total = dot(nbuf[1], wbuf[0, :, cut], ((1,), (0,)))
        total = total + dot(nbuf[2], wbuf[1, :, cut], ((1,), (0,)))
        pbuf[0:base, cut] = total[0:base].astype(BF16)
        if last:
            blank = jnp.zeros((EXTRA - over, step), F32)
            for s in range(plane):
                more = total[base + s * over : base + (s + 1) * over]
                more = jnp.concatenate([more, blank], axis=0).astype(BF16)
                pbuf[base + s * EXTRA : base + (s + 1) * EXTRA, cut] = more
    for s in range(plane):
        stores.append(
            pltpu.make_async_copy(
                pbuf.at[pl.ds(s * main, main), :],
                parts[s].at[pl.ds(0, main), :],
                p_sem.at[0, s],
            )
        )
        stores[-1].start()
        if last:
            stores.append(
                pltpu.make_async_copy(
                    pbuf.at[pl.ds(base + s * EXTRA, EXTRA), :],
                    parts[s].at[pl.ds(main, EXTRA), :],
                    p_sem.at[1, s],
                )
            )
            stores[-1].start()

    def lanes(column, shift, width=128):
        shape = (column.shape[0], width)
        row = lax.broadcasted_iota(jnp.int32, shape, 0) + shift
        lane = lax.broadcasted_iota(jnp.int32, shape, 1)
        return jnp.sum(jnp.where(row == lane, column, 0.0), axis=0, keepdims=True)

    own = [lanes(score[s * main : (s + 1) * main], 0) for s in range(plane)]
    if not last:
        score_ref[...] = jnp.concatenate(own, axis=0)
    else:
        lane = lax.broadcasted_iota(jnp.int32, (1, 128), 1)
        over_rows = [
            lanes(score[base + s * over : base + (s + 1) * over], main) for s in range(plane)
        ]
        for r in range(LINE):
            for s in range(plane):
                value = own[s] if r == LINE - 1 else earlier[r][s : s + 1, :]
                for j in range(OVER):
                    at = main + OVER * r + j
                    one = jnp.sum(jnp.where(lane == at, over_rows[s], 0.0), axis=1, keepdims=True)
                    value = jnp.where(lane == main + j, one, value)
                score_ref[r * plane + s : r * plane + s + 1, :] = value
    for copy in stores:
        copy.wait()


def expert(ins, weights, main, earlier, after):
    plane = len(ins)
    width = ins[0].shape[1]
    last = len(earlier) > 0
    hid = weights[0].shape[1]
    base, over = plane * main, LINE * OVER
    rows = base + (plane * over if last else 0)
    spread = base + (plane * EXTRA if last else 0)
    tile = 256 if hid % 256 == 0 else hid
    height = main + (EXTRA if last else 0)
    scratch = [
        pltpu.VMEM((rows, width), BF16),
        pltpu.VMEM((rows, width), BF16),
        pltpu.VMEM((3, hid, width), BF16),
        pltpu.VMEM((3, rows, hid), BF16),
        pltpu.VMEM((spread, width), BF16),
        pltpu.SemaphoreType.DMA((2, plane)),
        pltpu.SemaphoreType.DMA((3, hid // tile)),
        pltpu.SemaphoreType.DMA((3,)),
        pltpu.SemaphoreType.DMA((2, plane)),
    ]
    shapes = [like((height, width))] * plane + [like((rows, hid))] * 3
    shapes += [like((LINE * plane if last else plane, 128), F32)]
    specs = [hbm()] * (plane + 3) + [whole()]
    if last:
        scratch += [
            pltpu.VMEM((plane * EXTRA, width), BF16),
            pltpu.SemaphoreType.DMA((plane,)),
            pltpu.SemaphoreType.DMA((2,)),
        ]
        shapes += [like((plane * over, width))] * 2
        specs += [hbm()] * 2
    out = call(
        functools.partial(expert_kernel, plane, main, tile, last),
        [*ins, *weights, *earlier],
        [hbm()] * (plane + 3) + [whole()] * len(earlier),
        shapes,
        specs,
        after,
        10.0,
        scratch,
        60 if last else 32,
    )
    return out[:plane], out[plane : plane + 3], out[plane + 3], out[plane + 4 :]


def weight_kernel(plane, main, chunks, tailed, addends, half_ref, *refs):
    messages, refs = refs[: plane * chunks], refs[plane * chunks :]
    narrow = [refs[r * 3 : (r + 1) * 3] for r in range(chunks)]
    refs = refs[3 * chunks :]
    tails, refs = refs[:tailed], refs[tailed:]
    more, refs = refs[:addends], refs[addends:]
    scratch = refs[-7 - (2 if addends else 0) :]
    outs = refs[: len(refs) - len(scratch)]
    rows_x, rows_s, nbuf, obuf, m_sem, n_sem, out_sem = scratch[:7]
    units, width = obuf.shape[1:]
    first = pl.multiple_of(half_ref[0] * units, units)

    def load(i):
        copies, at = [], 0
        for r in range(chunks):
            size = narrow[r][i].shape[0]
            copies.append(
                pltpu.make_async_copy(
                    narrow[r][i].at[:, pl.ds(first, units)],
                    nbuf.at[i, pl.ds(at, size), :],
                    n_sem.at[i, r],
                )
            )
            at += size
        return copies

    def load_rows(i, target):
        copies, at = [], 0
        for k, message in enumerate(messages):
            copies.append(
                pltpu.make_async_copy(
                    message.at[pl.ds(i * main, main), :],
                    target.at[pl.ds(at, main), :],
                    m_sem.at[i, k],
                )
            )
            at += main
        if tailed:
            copies.append(
                pltpu.make_async_copy(
                    tails[i], target.at[pl.ds(at, tails[i].shape[0]), :], m_sem.at[i, len(messages)]
                )
            )
        return copies

    order = (1, 2, 0)
    loads = [load(1) + load_rows(0, rows_x), load(2), load(0) + load_rows(1, rows_s)]
    if addends:
        abuf, a_sem = scratch[7:]
        for k in range(addends):
            for place in range(3):
                source = more[k].at[place, pl.ds(first, units), :] if k == 0 else more[k].at[place]
                loads[place].append(
                    pltpu.make_async_copy(source, abuf.at[k, place], a_sem.at[k, place])
                )
    for copies in loads:
        for copy in copies:
            copy.start()
    stores = []
    step = min(width, 512)
    for place, i in enumerate(order):
        for copy in loads[place]:
            copy.wait()
        right = rows_s if i == 0 else rows_x
        for n in range(0, width, step):
            cut = slice(n, n + step)
            total = dot(nbuf[i], right[:, cut], ((0,), (0,)))
            for k in range(addends):
                total = total + abuf[k, place, :, cut].astype(F32)
            obuf[place, :, cut] = total.astype(BF16)
        target = outs[place].at[0] if len(outs) == 3 else outs[0].at[place]
        stores.append(pltpu.make_async_copy(obuf.at[place], target, out_sem.at[place]))
        stores[-1].start()
    for copy in stores:
        copy.wait()


def weight_grads(half, messages, narrow, tails, more, main, units, split, micros, after):
    plane, chunks = len(messages[0]), len(messages)
    rows = chunks * plane * main + (tails[0].shape[0] if tails else 0)
    width = messages[0][0].shape[1]
    shapes = [(1, units, width)] * 3 if split else [(3, units, width)]
    scratch = [
        pltpu.VMEM((rows, width), BF16),
        pltpu.VMEM((rows, width), BF16),
        pltpu.VMEM((3, rows, units), BF16),
        pltpu.VMEM((3, units, width), BF16),
        pltpu.SemaphoreType.DMA((2, chunks * plane + 1)),
        pltpu.SemaphoreType.DMA((3, chunks)),
        pltpu.SemaphoreType.DMA((3,)),
    ]
    if more:
        scratch += [
            pltpu.VMEM((len(more), 3, units, width), BF16),
            pltpu.SemaphoreType.DMA((len(more), 3)),
        ]
    given = [a for m in messages for a in m] + [a for n in narrow for a in n]
    given += [*tails, *more]
    return call(
        functools.partial(weight_kernel, plane, main, chunks, len(tails), len(more)),
        [half, *given],
        [smem()] + [hbm()] * len(given),
        [like(s) for s in shapes],
        [hbm()] * len(shapes),
        after,
        micros,
        scratch,
        60 if more else 50,
    )


def scatter_kernel(plane, main, r, added, last, place_ref, prob_ref, *refs):
    backs, refs = refs[:plane], refs[plane:]
    tails, refs = refs[:plane], refs[plane:]
    more_in, refs = refs[:added], refs[added:]
    if last:
        dlogits_ref, router_ref, refs = refs[0], refs[1], refs[2:]
    out_ref, rows_ref, more_ref, rank_ref, sems = refs
    copies = []
    for s in range(plane):
        copies.append(
            pltpu.make_async_copy(
                backs[s].at[pl.ds(0, main), :], rows_ref.at[pl.ds(s * main, main), :], sems.at[0, s]
            )
        )
        copies.append(
            pltpu.make_async_copy(
                tails[s].at[pl.ds(main, EXTRA), :],
                more_ref.at[pl.ds(s * EXTRA, EXTRA), :],
                sems.at[1, s],
            )
        )
    for copy in copies:
        copy.start()
    z, q = place_ref[0], place_ref[1]
    rank_ref[...] = rank_of(prob_ref[...])
    picks, more = [], []
    for s in range(plane):
        rank_row = rank_ref[pl.ds(z * plane + (q ^ s), 1), :]
        picks.append(slots(rank_row, main))
        more.append(extra_slots(rank_row, main, r, 0))
    for copy in copies:
        copy.wait()
    total = dot(jnp.concatenate(picks, axis=0).astype(BF16), rows_ref[...], ((0,), (0,)))
    total = total + dot(jnp.concatenate(more, axis=0).astype(BF16), more_ref[...], ((0,), (0,)))
    for ref in more_in:
        total = total + ref[...].astype(F32)
    if last:
        total = total + dot(dlogits_ref[...], router_ref[...], ((0,), (0,)))
    out_ref[...] = total.astype(BF16)


def scatter(place, prob, backs, tails, main, r, added, router, after):
    plane = len(backs)
    width = backs[0].shape[1]
    experts, count = prob.shape
    operands = [place, prob, *backs, *tails, *added, *router]
    return call(
        functools.partial(scatter_kernel, plane, main, r, len(added), len(router) > 0),
        operands,
        [smem(), whole()] + [hbm()] * (2 * plane) + [whole()] * (len(added) + len(router)),
        like((count, width)),
        whole(),
        after,
        2.5,
        [
            pltpu.VMEM((plane * main, width), BF16),
            pltpu.VMEM((plane * EXTRA, width), BF16),
            pltpu.VMEM((experts, count), F32),
            pltpu.SemaphoreType.DMA((2, plane)),
        ],
        60 if r < 3 else 16,
    )


def router_kernel(prob_ref, score_ref, x_ref, dlogits_ref, term_ref, dense_ref):
    prob = prob_ref[...]
    rank = rank_of(prob)
    member = prob >= 0.0
    score = score_ref[...]
    high = score.astype(BF16)
    rest = score - high.astype(F32)
    mid = rest.astype(BF16)
    low = (rest - mid.astype(F32)).astype(BF16)
    for e in range(prob.shape[0]):
        pick = slots(rank[e : e + 1, :], score.shape[1]).astype(BF16)
        value = dot(high[e : e + 1, :], pick, ((1,), (0,)))
        value = value + dot(mid[e : e + 1, :], pick, ((1,), (0,)))
        dense_ref[e : e + 1, :] = value + dot(low[e : e + 1, :], pick, ((1,), (0,)))
    weighted = dense_ref[...]
    both = weighted - prob * jnp.sum(weighted, axis=0, keepdims=True)
    dlogits = jnp.where(member, both, 0.0).astype(BF16)
    dlogits_ref[...] = dlogits
    term_ref[...] = dot(dlogits, x_ref[...], ((1,), (0,)))


def router_grads(prob, score, x):
    experts, count = prob.shape
    width = x.shape[1]
    return call(
        router_kernel,
        [prob, score, x],
        [whole()] * 3,
        [like((experts, count)), like((experts, width), F32)],
        [whole()] * 2,
        (),
        2.5,
        [pltpu.VMEM((experts, count), F32)],
    )


def local(tokens_in, grad_out, routes, router_weight, w_gate, w_up, w_down):
    count, width = tokens_in.shape
    experts = router_weight.shape[1]
    main = count * routes.shape[1] // experts
    plane = experts // LINE
    me = lax.axis_index("expert")
    z, q = me // plane, me % plane
    end = ((z == 0) | (z == LINE - 1)).astype(jnp.int32)
    place = jnp.stack([z, q, end]).astype(jnp.int32)
    router_t = router_weight.T

    def line(pairs):
        return [(a * plane + i, b * plane + i) for a, b in pairs for i in range(plane)]

    pair_swap = line([(0, 1), (1, 0), (2, 3), (3, 2)])
    mid_swap = line([(1, 2), (2, 1)])
    outward = line([(1, 0), (2, 3)])
    inward = line([(0, 1), (3, 2)])
    send = lambda a, perm: lax.ppermute(a, "expert", perm)
    across = lambda a, bit: send(a, [(i, i ^ bit) for i in range(experts)])

    prob, own = call(
        gate_kernel,
        [routes.T, tokens_in, grad_out, router_t],
        [whole()] * 4,
        [like((experts, count), F32), like((2 * count + group(experts), width))],
        [whole()] * 2,
        (),
        3.0,
        limit=60,
    )
    near, mid = send(own, pair_swap), send(own, mid_swap)
    near2, mid2 = send(mid, outward), send(near, mid_swap)
    far = send(mid2, outward)
    cands = [(own,), (near,), (near2, mid2), (far, mid)]

    weights = (w_gate, w_up, w_down)
    messages, probs, parts, narrow, scores = [], [], [], [], []

    def pick_rows(r, tail, after):
        rows, block_prob, tail = compact(
            place, cands[r], tail, plane, experts, count, main, r, after
        )
        probs.append(block_prob)
        messages.append([rows[0]] + [across(rows[s], s) for s in range(1, plane)])
        return tail

    def run_expert(r, after):
        out = expert(messages[r], weights, main, scores if r == LINE - 1 else [], after)
        parts.append(out[0])
        narrow.append(out[1])
        scores.append(out[2])
        return out[3]

    tail = pick_rows(0, None, ())
    tail = pick_rows(1, tail, ())
    run_expert(0, (tail,))
    tail = pick_rows(2, tail, (scores[0],))
    run_expert(1, (tail,))
    tail = pick_rows(3, tail, (scores[1],))
    run_expert(2, (tail,))
    hid = w_gate.shape[1]
    units = hid // lax.axis_size("dp")
    half = lax.axis_index("dp").reshape(1).astype(jnp.int32)
    swap = [(i, 1 - i) for i in range(2)]
    (early,) = weight_grads(
        jnp.zeros_like(half), messages[: LINE - 1], narrow, (), (), main, hid, False, 11.0, ()
    )
    tails = run_expert(3, (early,))

    def tied(a, *others):
        return lax.optimization_barrier((a, *others))[0]

    back = [[parts[r][0]] + [across(parts[r][s], s) for s in range(1, plane)] for r in range(LINE)]
    join = lambda r, added, router, after: scatter(
        place, probs[r], back[r], back[-1], main, r, added, router, after
    )
    given = messages[-1:], narrow[-1:], tails
    (gone,) = weight_grads(1 - half, *given, (early,), main, units, False, 6.0, ())

    sum3 = join(3, [], (), (gone,))
    other = lax.ppermute(tied(gone, sum3), "dp", swap)
    packed = tied(scores[-1], sum3)[jnp.arange(experts) ^ me]
    score = lax.all_to_all(packed, "expert", split_axis=0, concat_axis=0, tiled=True)

    sum2 = join(2, [send(sum3, inward)], (), (score,))
    sum3 = (sum3.astype(F32) + send(sum2, inward).astype(F32)).astype(BF16)
    dlogits, term = router_grads(prob, tied(score, sum2), tokens_in)

    def tree(values):
        while len(values) > 1:
            values = [values[i] + values[i + 1] for i in range(0, len(values), 2)]
        return values[0]

    grads = weight_grads(half, *given, (early, other), main, units, True, 12.0, (sum2,))
    sum1 = join(1, [send(sum2, mid_swap)], (), (term, grads[0]))
    got = [send(sum1, pair_swap), send(sum3, mid_swap)]
    term = tied(term, sum1)
    term = tree([term] + [across(term, s) for s in range(1, plane)])
    term = tied(term, *got)
    grad_x = join(0, got, (dlogits, router_t), ())

    term = tree([term] + [across(term, r * plane) for r in range(1, LINE)])
    term = tied(term, grad_x)
    term = term + lax.ppermute(term, "dp", swap)
    grad_router = term.T / count
    return (grad_x, *grads, grad_router)


def solution(mesh):
    return jax.shard_map(
        local,
        mesh=mesh,
        in_specs=(
            P(("dp", "expert"), None),
            P(("dp", "expert"), None),
            P(("dp", "expert"), None),
            P(),
            P("expert", None, None),
            P("expert", None, None),
            P("expert", None, None),
        ),
        out_specs=(
            P(("dp", "expert"), None),
            P("expert", "dp", None),
            P("expert", "dp", None),
            P("expert", "dp", None),
            P(),
        ),
        check_vma=False,
    )
```

```python
import functools

import jax
import jax.numpy as jnp
from jax import lax
from jax.experimental import pallas as pl
from jax.experimental.pallas import tpu as pltpu
from jax.sharding import PartitionSpec as P

LINE = 4
OVER = 2
EXTRA = 16
MIB = 1 << 20
SPEED = 1.1e9
F32 = jnp.float32
BF16 = jnp.bfloat16


def dot(a, b, contract):
    return lax.dot_general(a, b, (contract, ((), ())), preferred_element_type=F32)


def hbm():
    return pl.BlockSpec(memory_space=pl.ANY)


def whole():
    return pl.BlockSpec(memory_space=pltpu.VMEM)


def smem():
    return pl.BlockSpec(memory_space=pltpu.SMEM)


def call(kernel, operands, in_specs, out_shape, out_specs, after, micros, scratch=(), limit=16):
    count, more = len(operands), len(after)

    def body(*refs):
        kernel(*refs[:count], *refs[count + more :])

    return pl.pallas_call(
        body,
        out_shape=out_shape,
        in_specs=list(in_specs) + [hbm()] * more,
        out_specs=out_specs,
        scratch_shapes=scratch,
        compiler_params=pltpu.CompilerParams(vmem_limit_bytes=limit * MIB),
        cost_estimate=pl.CostEstimate(
            flops=int(micros * SPEED), bytes_accessed=1024, transcendentals=0
        ),
    )(*operands, *after)


def like(shape, kind=BF16):
    return jax.ShapeDtypeStruct(shape, kind)


def group(size):
    return -(-size // 16) * 16


def gate_kernel(routes_ref, x_ref, g_ref, router_ref, prob_ref, out_ref):
    logits = dot(router_ref[...], x_ref[...], ((1,), (1,)))
    row = lax.broadcasted_iota(jnp.int32, logits.shape, 0)
    member = row == routes_ref[0:1, :]
    for k in range(1, routes_ref.shape[0]):
        member = member | (row == routes_ref[k : k + 1, :])
    top = jnp.max(jnp.where(member, logits, -jnp.inf), axis=0, keepdims=True)
    weight = jnp.where(member, jnp.exp(logits - top), 0.0)
    prob = jnp.where(member, weight / jnp.sum(weight, axis=0, keepdims=True), -1.0)
    prob_ref[...] = prob
    experts, count = prob.shape
    out_ref[0:count, :] = x_ref[...]
    out_ref[count : 2 * count, :] = g_ref[...]
    rest = prob
    for k in range(3):
        piece = rest.astype(BF16)
        rest = rest - piece.astype(F32)
        out_ref[2 * count : 2 * count + experts, k * count : (k + 1) * count] = piece
    tail = out_ref.shape[1] - 3 * count
    out_ref[2 * count : 2 * count + experts, 3 * count :] = jnp.zeros((experts, tail), BF16)


def rank_of(prob):
    count = prob.shape[1]
    earlier = lax.broadcasted_iota(jnp.int32, (count, count), 0) < lax.broadcasted_iota(
        jnp.int32, (count, count), 1
    )
    member = prob >= 0.0
    rank = dot(member.astype(F32).astype(BF16), earlier.astype(F32).astype(BF16), ((1,), (0,)))
    return jnp.where(member, rank, -1.0)


def slots(rank_row, count):
    row = lax.broadcasted_iota(jnp.int32, (count, rank_row.shape[1]), 0).astype(F32)
    return (row == rank_row).astype(F32)


def extra_slots(rank_row, main, r, shift):
    row = lax.broadcasted_iota(jnp.int32, (EXTRA, rank_row.shape[1]), 0).astype(F32)
    row = row - float(shift + OVER * r)
    return ((row >= 0.0) & (row < OVER) & (row + main == rank_row)).astype(F32)


def compact_kernel(plane, main, r, cands, place_ref, *refs):
    z, q, end = place_ref[0], place_ref[1], place_ref[2]
    given, refs = refs[:cands], refs[cands:]
    if r > 0:
        tail_in, refs = refs[0], refs[1:]
    outs, refs = refs[:plane], refs[plane:]
    prob_ref, tail_ref, rank_ref = refs
    experts, count = prob_ref.shape
    block = given[0][...]
    if cands == 2:
        block = jnp.where(end > 0, block, given[1][...])
    rows_x, rows_s = block[0:count], block[count : 2 * count]
    pieces = [
        block[2 * count : 2 * count + experts, k * count : (k + 1) * count].astype(F32)
        for k in range(3)
    ]
    prob_ref[...] = (pieces[0] + pieces[1]) + pieces[2]
    rank_ref[...] = rank_of(prob_ref[...])
    picks, more_x, more_s, factor, more_factor = [], [], [], [], []
    for s in range(plane):
        expert = z * plane + (q ^ s)
        rank_row = rank_ref[pl.ds(expert, 1), :]
        prob_row = prob_ref[pl.ds(expert, 1), :]
        picks.append(slots(rank_row, main))
        more_x.append(extra_slots(rank_row, main, r, 0))
        more_s.append(extra_slots(rank_row, main, r, LINE * OVER))
        factor.append(jnp.sum(picks[-1] * prob_row, axis=1, keepdims=True))
        more_factor.append(jnp.sum(more_s[-1] * prob_row, axis=1, keepdims=True))
    pick = jnp.concatenate(picks, axis=0).astype(BF16)
    value_x = dot(pick, rows_x, ((1,), (0,)))
    value_s = dot(pick, rows_s, ((1,), (0,))) * jnp.concatenate(factor, axis=0)
    tail = dot(jnp.concatenate(more_x, axis=0).astype(BF16), rows_x, ((1,), (0,)))
    tail_s = dot(jnp.concatenate(more_s, axis=0).astype(BF16), rows_s, ((1,), (0,)))
    tail = tail + tail_s * jnp.concatenate(more_factor, axis=0)
    if r > 0:
        tail = tail + tail_in[...].astype(F32)
    tail_ref[...] = tail.astype(BF16)
    for s in range(plane):
        part = slice(s * main, (s + 1) * main)
        outs[s][0:main, :] = value_x[part].astype(BF16)
        outs[s][main : 2 * main, :] = value_s[part].astype(BF16)
        if r == LINE - 1:
            outs[s][2 * main :, :] = tail[s * EXTRA : (s + 1) * EXTRA].astype(BF16)


def compact(place, cands, tail, plane, experts, count, main, r, after):
    width = cands[0].shape[1]
    height = 2 * main + (EXTRA if r == LINE - 1 else 0)
    operands = [place, *cands] + ([] if tail is None else [tail])
    out = call(
        functools.partial(compact_kernel, plane, main, r, len(cands)),
        operands,
        [smem()] + [whole()] * (len(operands) - 1),
        [like((height, width))] * plane
        + [like((experts, count), F32), like((plane * EXTRA, width))],
        [whole()] * (plane + 2),
        after,
        3.0,
        [pltpu.VMEM((experts, count), F32)],
    )
    return out[:plane], out[plane], out[plane + 1]


def expert_kernel(plane, main, tile, last, *refs):
    ins, weights, refs = refs[:plane], refs[plane : plane + 3], refs[plane + 3 :]
    if last:
        earlier, refs = refs[: LINE - 1], refs[LINE - 1 :]
    parts, narrow, score_ref = refs[:plane], refs[plane : plane + 3], refs[plane + 3]
    refs = refs[plane + 4 :]
    if last:
        tails, refs = refs[:2], refs[2:]
        ebuf, e_sem, t_sem = refs[-3:]
    rows_x, rows_s, wbuf, nbuf, pbuf, row_sem, w_sem, n_sem, p_sem = refs[:9]
    hid, width = wbuf.shape[1:]
    tiles = hid // tile
    base = plane * main
    over = LINE * OVER

    row_copies, scaled_copies = [], []
    for s in range(plane):
        own = pl.ds(s * main, main)
        for i, target in enumerate((rows_x, rows_s)):
            (row_copies, scaled_copies)[i].append(
                pltpu.make_async_copy(
                    ins[s].at[pl.ds(i * main, main), :], target.at[own, :], row_sem.at[i, s]
                )
            )
        if last:
            row_copies.append(
                pltpu.make_async_copy(
                    ins[s].at[pl.ds(2 * main, EXTRA), :],
                    ebuf.at[pl.ds(s * EXTRA, EXTRA), :],
                    e_sem.at[s],
                )
            )
    w_copies = [
        [
            pltpu.make_async_copy(
                weights[i].at[0, pl.ds(f * tile, tile), :],
                wbuf.at[i, pl.ds(f * tile, tile), :],
                w_sem.at[i, f],
            )
            for i in range(3)
        ]
        for f in range(tiles)
    ]
    for copy in row_copies + w_copies[0][:2] + scaled_copies + w_copies[0][2:]:
        copy.start()
    for part in w_copies[1:]:
        for copy in part:
            copy.start()
    for copy in row_copies:
        copy.wait()
    stores = []
    if last:
        extra = ebuf[...].astype(F32)
        first = [extra[s * EXTRA : s * EXTRA + over] for s in range(plane)]
        second = [extra[s * EXTRA + over : s * EXTRA + 2 * over] for s in range(plane)]
        rows_x[base:, :] = jnp.concatenate(first, axis=0).astype(BF16)
        rows_s[base:, :] = jnp.concatenate(second, axis=0).astype(BF16)
        for i, source in enumerate((rows_x, rows_s)):
            stores.append(
                pltpu.make_async_copy(
                    source.at[pl.ds(base, plane * over), :], tails[i], t_sem.at[i]
                )
            )
            stores[-1].start()

    score = jnp.zeros((rows_x.shape[0], 1), F32)
    for f in range(tiles):
        cut = slice(f * tile, (f + 1) * tile)
        w_copies[f][0].wait()
        pre_gate = dot(rows_x[...], wbuf[0, cut, :], ((1,), (1,)))
        w_copies[f][1].wait()
        pre_up = dot(rows_x[...], wbuf[1, cut, :], ((1,), (1,)))
        for copy in (scaled_copies if f == 0 else []) + w_copies[f][2:]:
            copy.wait()
        grad_hidden = dot(rows_s[...], wbuf[2, cut, :], ((1,), (1,)))
        sig = jax.nn.sigmoid(pre_gate)
        act = pre_gate * sig
        hidden = (act * pre_up).astype(BF16)
        nbuf[0, :, cut] = hidden
        nbuf[1, :, cut] = (grad_hidden * pre_up * sig * (1.0 + pre_gate * (1.0 - sig))).astype(BF16)
        nbuf[2, :, cut] = (grad_hidden * act).astype(BF16)
        score = score + jnp.sum(hidden.astype(F32) * grad_hidden, axis=1, keepdims=True)
    for i in range(3):
        stores.append(pltpu.make_async_copy(nbuf.at[i], narrow[i], n_sem.at[i]))
        stores[-1].start()
    step = min(width, 512)
    for n in range(0, width, step):
        cut = slice(n, n + step)
        total = dot(nbuf[1], wbuf[0, :, cut], ((1,), (0,)))
        total = total + dot(nbuf[2], wbuf[1, :, cut], ((1,), (0,)))
        pbuf[0:base, cut] = total[0:base].astype(BF16)
        if last:
            blank = jnp.zeros((EXTRA - over, step), F32)
            for s in range(plane):
                more = total[base + s * over : base + (s + 1) * over]
                more = jnp.concatenate([more, blank], axis=0).astype(BF16)
                pbuf[base + s * EXTRA : base + (s + 1) * EXTRA, cut] = more
    for s in range(plane):
        stores.append(
            pltpu.make_async_copy(
                pbuf.at[pl.ds(s * main, main), :],
                parts[s].at[pl.ds(0, main), :],
                p_sem.at[0, s],
            )
        )
        stores[-1].start()
        if last:
            stores.append(
                pltpu.make_async_copy(
                    pbuf.at[pl.ds(base + s * EXTRA, EXTRA), :],
                    parts[s].at[pl.ds(main, EXTRA), :],
                    p_sem.at[1, s],
                )
            )
            stores[-1].start()

    def lanes(column, shift, width=128):
        shape = (column.shape[0], width)
        row = lax.broadcasted_iota(jnp.int32, shape, 0) + shift
        lane = lax.broadcasted_iota(jnp.int32, shape, 1)
        return jnp.sum(jnp.where(row == lane, column, 0.0), axis=0, keepdims=True)

    own = [lanes(score[s * main : (s + 1) * main], 0) for s in range(plane)]
    if not last:
        score_ref[...] = jnp.concatenate(own, axis=0)
    else:
        lane = lax.broadcasted_iota(jnp.int32, (1, 128), 1)
        over_rows = [
            lanes(score[base + s * over : base + (s + 1) * over], main) for s in range(plane)
        ]
        for r in range(LINE):
            for s in range(plane):
                value = own[s] if r == LINE - 1 else earlier[r][s : s + 1, :]
                for j in range(OVER):
                    at = main + OVER * r + j
                    one = jnp.sum(jnp.where(lane == at, over_rows[s], 0.0), axis=1, keepdims=True)
                    value = jnp.where(lane == main + j, one, value)
                score_ref[r * plane + s : r * plane + s + 1, :] = value
    for copy in stores:
        copy.wait()


def expert(ins, weights, main, earlier, after):
    plane = len(ins)
    width = ins[0].shape[1]
    last = len(earlier) > 0
    hid = weights[0].shape[1]
    base, over = plane * main, LINE * OVER
    rows = base + (plane * over if last else 0)
    spread = base + (plane * EXTRA if last else 0)
    tile = 256 if hid % 256 == 0 else hid
    height = main + (EXTRA if last else 0)
    scratch = [
        pltpu.VMEM((rows, width), BF16),
        pltpu.VMEM((rows, width), BF16),
        pltpu.VMEM((3, hid, width), BF16),
        pltpu.VMEM((3, rows, hid), BF16),
        pltpu.VMEM((spread, width), BF16),
        pltpu.SemaphoreType.DMA((2, plane)),
        pltpu.SemaphoreType.DMA((3, hid // tile)),
        pltpu.SemaphoreType.DMA((3,)),
        pltpu.SemaphoreType.DMA((2, plane)),
    ]
    shapes = [like((height, width))] * plane + [like((rows, hid))] * 3
    shapes += [like((LINE * plane if last else plane, 128), F32)]
    specs = [hbm()] * (plane + 3) + [whole()]
    if last:
        scratch += [
            pltpu.VMEM((plane * EXTRA, width), BF16),
            pltpu.SemaphoreType.DMA((plane,)),
            pltpu.SemaphoreType.DMA((2,)),
        ]
        shapes += [like((plane * over, width))] * 2
        specs += [hbm()] * 2
    out = call(
        functools.partial(expert_kernel, plane, main, tile, last),
        [*ins, *weights, *earlier],
        [hbm()] * (plane + 3) + [whole()] * len(earlier),
        shapes,
        specs,
        after,
        10.0,
        scratch,
        60 if last else 32,
    )
    return out[:plane], out[plane : plane + 3], out[plane + 3], out[plane + 4 :]


def weight_kernel(plane, main, chunks, tailed, addends, half_ref, *refs):
    messages, refs = refs[: plane * chunks], refs[plane * chunks :]
    narrow = [refs[r * 3 : (r + 1) * 3] for r in range(chunks)]
    refs = refs[3 * chunks :]
    tails, refs = refs[:tailed], refs[tailed:]
    more, refs = refs[:addends], refs[addends:]
    scratch = refs[-7 - (2 if addends else 0) :]
    outs = refs[: len(refs) - len(scratch)]
    rows_x, rows_s, nbuf, obuf, m_sem, n_sem, out_sem = scratch[:7]
    units, width = obuf.shape[1:]
    first = pl.multiple_of(half_ref[0] * units, units)

    def load(i):
        copies, at = [], 0
        for r in range(chunks):
            size = narrow[r][i].shape[0]
            copies.append(
                pltpu.make_async_copy(
                    narrow[r][i].at[:, pl.ds(first, units)],
                    nbuf.at[i, pl.ds(at, size), :],
                    n_sem.at[i, r],
                )
            )
            at += size
        return copies

    def load_rows(i, target):
        copies, at = [], 0
        for k, message in enumerate(messages):
            copies.append(
                pltpu.make_async_copy(
                    message.at[pl.ds(i * main, main), :],
                    target.at[pl.ds(at, main), :],
                    m_sem.at[i, k],
                )
            )
            at += main
        if tailed:
            copies.append(
                pltpu.make_async_copy(
                    tails[i], target.at[pl.ds(at, tails[i].shape[0]), :], m_sem.at[i, len(messages)]
                )
            )
        return copies

    order = (1, 2, 0)
    loads = [load(1) + load_rows(0, rows_x), load(2), load(0) + load_rows(1, rows_s)]
    if addends:
        abuf, a_sem = scratch[7:]
        for k in range(addends):
            for place in range(3):
                source = more[k].at[place, pl.ds(first, units), :] if k == 0 else more[k].at[place]
                loads[place].append(
                    pltpu.make_async_copy(source, abuf.at[k, place], a_sem.at[k, place])
                )
    for copies in loads:
        for copy in copies:
            copy.start()
    stores = []
    step = min(width, 512)
    for place, i in enumerate(order):
        for copy in loads[place]:
            copy.wait()
        right = rows_s if i == 0 else rows_x
        for n in range(0, width, step):
            cut = slice(n, n + step)
            total = dot(nbuf[i], right[:, cut], ((0,), (0,)))
            for k in range(addends):
                total = total + abuf[k, place, :, cut].astype(F32)
            obuf[place, :, cut] = total.astype(BF16)
        target = outs[place].at[0] if len(outs) == 3 else outs[0].at[place]
        stores.append(pltpu.make_async_copy(obuf.at[place], target, out_sem.at[place]))
        stores[-1].start()
    for copy in stores:
        copy.wait()


def weight_grads(half, messages, narrow, tails, more, main, units, split, micros, after):
    plane, chunks = len(messages[0]), len(messages)
    rows = chunks * plane * main + (tails[0].shape[0] if tails else 0)
    width = messages[0][0].shape[1]
    shapes = [(1, units, width)] * 3 if split else [(3, units, width)]
    scratch = [
        pltpu.VMEM((rows, width), BF16),
        pltpu.VMEM((rows, width), BF16),
        pltpu.VMEM((3, rows, units), BF16),
        pltpu.VMEM((3, units, width), BF16),
        pltpu.SemaphoreType.DMA((2, chunks * plane + 1)),
        pltpu.SemaphoreType.DMA((3, chunks)),
        pltpu.SemaphoreType.DMA((3,)),
    ]
    if more:
        scratch += [
            pltpu.VMEM((len(more), 3, units, width), BF16),
            pltpu.SemaphoreType.DMA((len(more), 3)),
        ]
    given = [a for m in messages for a in m] + [a for n in narrow for a in n]
    given += [*tails, *more]
    return call(
        functools.partial(weight_kernel, plane, main, chunks, len(tails), len(more)),
        [half, *given],
        [smem()] + [hbm()] * len(given),
        [like(s) for s in shapes],
        [hbm()] * len(shapes),
        after,
        micros,
        scratch,
        60 if more else 50,
    )


def scatter_kernel(plane, main, r, added, last, place_ref, prob_ref, *refs):
    backs, refs = refs[:plane], refs[plane:]
    tails, refs = refs[:plane], refs[plane:]
    more_in, refs = refs[:added], refs[added:]
    if last:
        dlogits_ref, router_ref, refs = refs[0], refs[1], refs[2:]
    out_ref, rows_ref, more_ref, rank_ref, sems = refs
    copies = []
    for s in range(plane):
        copies.append(
            pltpu.make_async_copy(
                backs[s].at[pl.ds(0, main), :], rows_ref.at[pl.ds(s * main, main), :], sems.at[0, s]
            )
        )
        copies.append(
            pltpu.make_async_copy(
                tails[s].at[pl.ds(main, EXTRA), :],
                more_ref.at[pl.ds(s * EXTRA, EXTRA), :],
                sems.at[1, s],
            )
        )
    for copy in copies:
        copy.start()
    z, q = place_ref[0], place_ref[1]
    rank_ref[...] = rank_of(prob_ref[...])
    picks, more = [], []
    for s in range(plane):
        rank_row = rank_ref[pl.ds(z * plane + (q ^ s), 1), :]
        picks.append(slots(rank_row, main))
        more.append(extra_slots(rank_row, main, r, 0))
    for copy in copies:
        copy.wait()
    total = dot(jnp.concatenate(picks, axis=0).astype(BF16), rows_ref[...], ((0,), (0,)))
    total = total + dot(jnp.concatenate(more, axis=0).astype(BF16), more_ref[...], ((0,), (0,)))
    for ref in more_in:
        total = total + ref[...].astype(F32)
    if last:
        total = total + dot(dlogits_ref[...], router_ref[...], ((0,), (0,)))
    out_ref[...] = total.astype(BF16)


def scatter(place, prob, backs, tails, main, r, added, router, after):
    plane = len(backs)
    width = backs[0].shape[1]
    experts, count = prob.shape
    operands = [place, prob, *backs, *tails, *added, *router]
    return call(
        functools.partial(scatter_kernel, plane, main, r, len(added), len(router) > 0),
        operands,
        [smem(), whole()] + [hbm()] * (2 * plane) + [whole()] * (len(added) + len(router)),
        like((count, width)),
        whole(),
        after,
        2.5,
        [
            pltpu.VMEM((plane * main, width), BF16),
            pltpu.VMEM((plane * EXTRA, width), BF16),
            pltpu.VMEM((experts, count), F32),
            pltpu.SemaphoreType.DMA((2, plane)),
        ],
        60 if r < 3 else 16,
    )


def router_kernel(prob_ref, score_ref, x_ref, dlogits_ref, term_ref, dense_ref):
    prob = prob_ref[...]
    rank = rank_of(prob)
    member = prob >= 0.0
    score = score_ref[...]
    high = score.astype(BF16)
    rest = score - high.astype(F32)
    mid = rest.astype(BF16)
    low = (rest - mid.astype(F32)).astype(BF16)
    for e in range(prob.shape[0]):
        pick = slots(rank[e : e + 1, :], score.shape[1]).astype(BF16)
        value = dot(high[e : e + 1, :], pick, ((1,), (0,)))
        value = value + dot(mid[e : e + 1, :], pick, ((1,), (0,)))
        dense_ref[e : e + 1, :] = value + dot(low[e : e + 1, :], pick, ((1,), (0,)))
    weighted = dense_ref[...]
    both = weighted - prob * jnp.sum(weighted, axis=0, keepdims=True)
    dlogits = jnp.where(member, both, 0.0).astype(BF16)
    dlogits_ref[...] = dlogits
    term_ref[...] = dot(dlogits, x_ref[...], ((1,), (0,)))


def router_grads(prob, score, x):
    experts, count = prob.shape
    width = x.shape[1]
    return call(
        router_kernel,
        [prob, score, x],
        [whole()] * 3,
        [like((experts, count)), like((experts, width), F32)],
        [whole()] * 2,
        (),
        2.5,
        [pltpu.VMEM((experts, count), F32)],
    )


def local(tokens_in, grad_out, routes, router_weight, w_gate, w_up, w_down):
    count, width = tokens_in.shape
    experts = router_weight.shape[1]
    main = count * routes.shape[1] // experts
    plane = experts // LINE
    me = lax.axis_index("expert")
    z, q = me // plane, me % plane
    end = ((z == 0) | (z == LINE - 1)).astype(jnp.int32)
    place = jnp.stack([z, q, end]).astype(jnp.int32)
    router_t = router_weight.T

    def line(pairs):
        return [(a * plane + i, b * plane + i) for a, b in pairs for i in range(plane)]

    pair_swap = line([(0, 1), (1, 0), (2, 3), (3, 2)])
    mid_swap = line([(1, 2), (2, 1)])
    outward = line([(1, 0), (2, 3)])
    inward = line([(0, 1), (3, 2)])
    send = lambda a, perm: lax.ppermute(a, "expert", perm)
    across = lambda a, bit: send(a, [(i, i ^ bit) for i in range(experts)])

    prob, own = call(
        gate_kernel,
        [routes.T, tokens_in, grad_out, router_t],
        [whole()] * 4,
        [like((experts, count), F32), like((2 * count + group(experts), width))],
        [whole()] * 2,
        (),
        3.0,
        limit=60,
    )
    near, mid = send(own, pair_swap), send(own, mid_swap)
    near2, mid2 = send(mid, outward), send(near, mid_swap)
    far = send(mid2, outward)
    cands = [(own,), (near,), (near2, mid2), (far, mid)]

    weights = (w_gate, w_up, w_down)
    messages, probs, parts, narrow, scores = [], [], [], [], []

    def pick_rows(r, tail, after):
        rows, block_prob, tail = compact(
            place, cands[r], tail, plane, experts, count, main, r, after
        )
        probs.append(block_prob)
        messages.append([rows[0]] + [across(rows[s], s) for s in range(1, plane)])
        return tail

    def run_expert(r, after):
        out = expert(messages[r], weights, main, scores if r == LINE - 1 else [], after)
        parts.append(out[0])
        narrow.append(out[1])
        scores.append(out[2])
        return out[3]

    tail = pick_rows(0, None, ())
    tail = pick_rows(1, tail, ())
    run_expert(0, (tail,))
    tail = pick_rows(2, tail, (scores[0],))
    run_expert(1, (tail,))
    tail = pick_rows(3, tail, (scores[1],))
    run_expert(2, (tail,))
    hid = w_gate.shape[1]
    units = hid // lax.axis_size("dp")
    half = lax.axis_index("dp").reshape(1).astype(jnp.int32)
    swap = [(i, 1 - i) for i in range(2)]
    (early,) = weight_grads(
        jnp.zeros_like(half), messages[: LINE - 1], narrow, (), (), main, hid, False, 11.0, ()
    )
    tails = run_expert(3, (early,))

    def tied(a, *others):
        return lax.optimization_barrier((a, *others))[0]

    back = [[parts[r][0]] + [across(parts[r][s], s) for s in range(1, plane)] for r in range(LINE)]
    join = lambda r, added, router, after: scatter(
        place, probs[r], back[r], back[-1], main, r, added, router, after
    )
    given = messages[-1:], narrow[-1:], tails
    (gone,) = weight_grads(1 - half, *given, (early,), main, units, False, 6.0, ())

    sum3 = join(3, [], (), (gone,))
    other = lax.ppermute(tied(gone, sum3), "dp", swap)
    packed = tied(scores[-1], sum3)[jnp.arange(experts) ^ me]
    score = lax.all_to_all(packed, "expert", split_axis=0, concat_axis=0, tiled=True)

    sum2 = join(2, [send(sum3, inward)], (), (score,))
    sum3 = (sum3.astype(F32) + send(sum2, inward).astype(F32)).astype(BF16)
    dlogits, term = router_grads(prob, tied(score, sum2), tokens_in)

    def tree(values):
        while len(values) > 1:
            values = [values[i] + values[i + 1] for i in range(0, len(values), 2)]
        return values[0]

    grads = weight_grads(half, *given, (early, other), main, units, True, 12.0, (sum2,))
    sum1 = join(1, [send(sum2, mid_swap)], (), (term, grads[0]))
    got = [send(sum1, pair_swap), send(sum3, mid_swap)]
    term = tied(term, sum1)
    term = tree([term] + [across(term, s) for s in range(1, plane)])
    term = tied(term, *got)
    grad_x = join(0, got, (dlogits, router_t), ())

    term = tree([term] + [across(term, r * plane) for r in range(1, LINE)])
    term = tied(term, grad_x)
    term = term + lax.ppermute(term, "dp", swap)
    grad_router = term.T / count
    return (grad_x, *grads, grad_router)


def solution(mesh):
    return jax.shard_map(
        local,
        mesh=mesh,
        in_specs=(
            P(("dp", "expert"), None),
            P(("dp", "expert"), None),
            P(("dp", "expert"), None),
            P(),
            P("expert", None, None),
            P("expert", None, None),
            P("expert", None, None),
        ),
        out_specs=(
            P(("dp", "expert"), None),
            P("expert", "dp", None),
            P("expert", "dp", None),
            P("expert", "dp", None),
            P(),
        ),
        check_vma=False,
    )
```
